128 devices in a mesh: feat: 16 (over z, y), grp: 8 (over x, core).
Axes of the slice: x: 4, y: 4, z: 4, core: 2. Of those that a mesh axis runs over, the one named last changes fastest.
Arguments:
- node_table: bfloat16 [8, 32768, 1024], P('grp', None, 'feat'), may hold values from -6 to 6
- node_ids: int32 [8, 32768], P('grp'), may hold values from 0 to 32767, as said below
- block_lists: int32 [8, 128, 3], P('grp'), may hold values from 0 to 255
- block_counts: int32 [8, 128], P('grp'), may hold values from 1 to 3
- tiles: bfloat16 [8, 128, 3, 128, 128], P('grp'), may hold values from 0.049804688 to 1
- batch_sizes: int32 [8], P('grp'), may hold values from 8192 to 16384, as said below
- w_self: bfloat16 [1024, 256], replicated, may hold values from -0.1875 to 0.1875
- w_neigh: bfloat16 [1024, 256], replicated, may hold values from -0.75 to 0.75
- bias: float32 [256], replicated, may hold values from -3 to 3
- cotangent: bfloat16 [8, 16384, 256], P('grp', 'feat'), may hold values from -0.06591797 to 0.06591797
Outputs:
- hidden: bfloat16 [8, 16384, 256], P('grp', 'feat')
- grad_self: float32 [1024, 256], P('feat')
- grad_neigh: float32 [1024, 256], P('feat')
The draws below stay inside these ranges and needn't reach their ends.
Inputs may be any that keep to these rules, and one draw needn't show every extreme that they name: `batch_sizes`: each group's entry is at least half of 16384; some group has exactly 16384. `node_ids`: each group's entries are a permutation of 0 to 32767 in which every aligned run of 128 entries (starting at a multiple of 128) holds exactly the rows of one aligned 128-row block of the table, in some order.
All inputs are finite; a program needn't handle non-finite values.
Results may differ from the reference program's by a relative error of at most 0.0052.
Values may be sent and summed in bfloat16 or wider, within the bound.
No kernel may reach another device: no remote copies, remote signals or barrier semaphores. Data moves between devices by JAX's collectives and lax.ppermute only.
A program may use at most 128 MiB of HBM per device.

```python
import jax
import jax.numpy as jnp
from jax import lax

F = 1024
H = 256
BLOCK = 128
MAXNB = 3
DST = 16384
SRC = 32768
DB = 128
NSB = 256
TOTAL = 131072
N_GRP = 8


def draw_batch_sizes(key, part):
    key = jax.random.fold_in(key, 7)
    first, second = jax.random.split(key)
    sizes = jax.random.randint(first, (N_GRP,), DST // 2, DST + 1, dtype=jnp.int32)
    fullest = jax.random.randint(second, (), 0, N_GRP, dtype=jnp.int32)
    return sizes.at[fullest].set(DST)


def draw_node_ids(key, part):
    key = jax.random.fold_in(key, 11)
    outer_key, inner_key = jax.random.split(key)
    order = jax.vmap(lambda k: jax.random.permutation(k, NSB))(jax.random.split(outer_key, N_GRP))
    inner = jax.vmap(lambda k: jax.random.permutation(k, BLOCK))(jax.random.split(inner_key, N_GRP * NSB))
    inner = inner.reshape(N_GRP, NSB, BLOCK).astype(jnp.int32)
    ids = order.astype(jnp.int32)[:, :, None] * BLOCK + inner
    return ids.reshape(N_GRP, SRC).astype(jnp.int32)


def with_ends(entries, stream_key, smallest, high):
    longest = entries.shape.index(max(entries.shape))
    spots = []
    for shift in (0, 1):
        where = [jax.random.randint(jax.random.fold_in(stream_key, axis), (), 0, length) for axis, length in enumerate(entries.shape)]
        where[longest] = (where[longest] + shift) % entries.shape[longest]
        spots.append(tuple(where))
    return entries.at[spots[0]].set(smallest).at[spots[1]].set(high)


def block_scale(stream_key, extent, pieces, low, largest):
    gain, own = 1.0, jax.random.fold_in(stream_key, 6)
    for axis_at, blocks in pieces:
        steps = jnp.exp(jax.random.uniform(jax.random.fold_in(own, axis_at), (blocks,), jnp.float32, low / len(pieces), largest / len(pieces)))
        gain = gain * jnp.repeat(steps, extent[axis_at] // blocks).reshape([-1 if axis == axis_at else 1 for axis in range(len(extent))])
    return gain


def scatter_about(own_key, dims, scale, limit, cuts=(), kind=jnp.bfloat16):
    entries = scale * jax.random.normal(own_key, dims, jnp.float32)
    if cuts:
        entries = entries * block_scale(own_key, dims, cuts, -0.22, 0.18)
    return jnp.clip(entries, -limit, limit).astype(kind)


def setup_inputs(seed: int = 0) -> dict:
    splits = jax.random.split(jax.random.key(seed), 11)
    return {
        "node_table": scatter_about(splits[0], (N_GRP, SRC, F), 1.0, 6.0, ((0, 8), (2, 16))),
        "node_ids": draw_node_ids(jax.random.fold_in(splits[10], 71), 0),
        "block_lists": with_ends(jax.random.randint(splits[2], (N_GRP, DB, MAXNB), 0, NSB), jax.random.fold_in(splits[2], 1), 0, NSB - 1).astype(jnp.int32),
        "block_counts": with_ends(jax.random.randint(splits[3], (N_GRP, DB), 1, MAXNB + 1), jax.random.fold_in(splits[3], 1), 1, MAXNB).astype(jnp.int32),
        "tiles": jnp.clip(0.049804688 + 0.9501953 * jax.random.uniform(splits[4], (N_GRP, DB, MAXNB, BLOCK, BLOCK), jnp.float32) ** block_scale(splits[4], (N_GRP, DB, MAXNB, BLOCK, BLOCK), ((0, 8),), -0.2, 0.2), 0.049804688, 1.0).astype(jnp.bfloat16),
        "batch_sizes": draw_batch_sizes(jax.random.fold_in(splits[10], 71), 0),
        "w_self": scatter_about(splits[6], (F, H), F ** -0.5, 0.1875),
        "w_neigh": scatter_about(splits[7], (F, H), (F // 16) ** -0.5, 0.75),
        "bias": scatter_about(splits[8], (H,), 0.5, 3.0, (), jnp.float32),
        "cotangent": scatter_about(splits[9], (N_GRP, DST, H), (4.0 / TOTAL ** 0.5), 0.06591797, ((0, 8), (1, 16))),
    }


def aggregate(source_rows, lists, counts, tiles):
    block = tiles.shape[-1]
    width = source_rows.shape[1]
    blocks = source_rows.reshape(-1, block, width)
    picked = blocks[lists]
    keeping = jnp.arange(lists.shape[1], dtype=jnp.int32)[None, :] < counts[:, None]
    weights = jnp.where(keeping[:, :, None, None], tiles, jnp.zeros((), tiles.dtype))
    summed = jnp.einsum('bsij,bsjc->bic', weights.astype(jnp.float32), picked.astype(jnp.float32))
    degree = lax.optimization_barrier(jnp.sum(weights.astype(jnp.float32), axis=(1, 3)))
    return (summed / degree[:, :, None]).reshape(-1, width).astype(jnp.bfloat16)

def one_group(args, w_self, w_neigh, bias):
    table, ids, lists, counts, tiles, size, upstream = args
    source_rows = table[ids]
    agg = aggregate(source_rows, lists, counts, tiles)
    own = source_rows[:agg.shape[0]]
    pre = jnp.dot(own, w_self, preferred_element_type=jnp.float32) + jnp.dot(agg, w_neigh, preferred_element_type=jnp.float32) + bias
    valid = (jnp.arange(agg.shape[0], dtype=jnp.int32) < size).astype(jnp.float32)[:, None]
    active, back = jax.vjp(jax.nn.gelu, pre)
    hidden = (active * valid).astype(jnp.bfloat16)
    slope = (back(upstream.astype(jnp.float32))[0] * valid).astype(jnp.bfloat16)
    grad_own = jnp.dot(own.T, slope, preferred_element_type=jnp.float32)
    grad_agg = jnp.dot(agg.T, slope, preferred_element_type=jnp.float32)
    return (hidden, grad_own, grad_agg)

def reference(node_table, node_ids, block_lists, block_counts, tiles, batch_sizes, w_self, w_neigh, bias, cotangent):
    hidden, grad_own, grad_agg = lax.map(lambda args: one_group(args, w_self, w_neigh, bias), (node_table, node_ids, block_lists, block_counts, tiles, batch_sizes, cotangent))
    return (hidden, lax.optimization_barrier(jnp.sum(grad_own, axis=0)), lax.optimization_barrier(jnp.sum(grad_agg, axis=0)))
```

```python
import jax
import jax.numpy as jnp
from jax import lax
from jax.experimental import pallas as pl
from jax.experimental.pallas import tpu as pltpu
from jax.sharding import Mesh, PartitionSpec as P

BLOCK = 128
MIB = 1 << 20
FEAT = ("z", "y")
GRP = ("x", "core")
NT = (((1,), (1,)), ((), ()))
NN = (((1,), (0,)), ((), ()))


def dot(left, right, dims=NN):
    return lax.dot_general(left, right, dims, preferred_element_type=jnp.float32)


def selector(within):
    rows = lax.broadcasted_iota(jnp.int32, (BLOCK, BLOCK), 0)
    return jnp.where(rows == within, 1.0, 0.0).astype(jnp.bfloat16)


def pick_kernel(which_ref, table_ref, out_ref, sem):
    owners, _, owned = out_ref.shape
    per = owned // BLOCK

    def start(b, carry):
        w = which_ref[b]
        pltpu.make_async_copy(
            table_ref.at[:, pl.ds(pl.multiple_of(w * BLOCK, BLOCK), BLOCK)],
            out_ref.at[b // per, :, pl.ds(pl.multiple_of((b % per) * BLOCK, BLOCK), BLOCK)],
            sem,
        ).start()
        return carry

    lax.fori_loop(0, owners * per, start, 0)
    pltpu.make_async_copy(out_ref, out_ref, sem).wait()


def pick(which, table, owners):
    width, rows = table.shape
    owned = rows // 2 // owners
    return pl.pallas_call(
        pick_kernel,
        out_shape=jax.ShapeDtypeStruct((owners, width, owned), table.dtype),
        in_specs=[pl.BlockSpec(memory_space=pltpu.SMEM), pl.BlockSpec(memory_space=pl.ANY)],
        out_specs=pl.BlockSpec(memory_space=pl.ANY),
        scratch_shapes=[pltpu.SemaphoreType.DMA],
        cost_estimate=pl.CostEstimate(flops=0, bytes_accessed=4 * MIB, transcendentals=0),
        name="pick_own_blocks",
    )(which, table)


def aggregate_kernel(which_ref, lists_ref, counts_ref, ids_ref, table_ref, tiles_ref, out_ref, source):
    step = pl.program_id(0)
    blocks = ids_ref.shape[0]
    width = table_ref.shape[0]
    per, slots = tiles_ref.shape[0], tiles_ref.shape[1]

    @pl.when(step == 0)
    def _():
        source[blocks] = jnp.zeros(source.shape[1:], source.dtype)

        def place(n, carry):
            w = which_ref[n]
            chosen = table_ref[:, pl.ds(pl.multiple_of(w * BLOCK, BLOCK), BLOCK)]
            within = ids_ref[pl.ds(n, 1), :] - w * BLOCK
            source[n, :width] = dot(chosen, selector(within)).astype(jnp.bfloat16)
            source[n, width:] = jnp.ones((source.shape[1] - width, BLOCK), jnp.bfloat16)
            return carry

        lax.fori_loop(0, blocks, place, 0, unroll=4)

    for b in range(per):
        d = step * per + b
        count = counts_ref[d]
        left = jnp.concatenate(
            [source[jnp.where(s < count, lists_ref[d * slots + s], blocks)] for s in range(slots)], axis=1
        )
        right = jnp.concatenate([tiles_ref[b, s] for s in range(slots)], axis=1)
        total = dot(left, right, NT)
        out_ref[0, :, b * BLOCK : (b + 1) * BLOCK] = (total[:width] / total[width : width + 1]).astype(jnp.bfloat16)


def aggregate(which, lists, counts, ids, table, tiles, owners):
    width, rows = table.shape
    blocks = rows // BLOCK
    dst_blocks, slots = tiles.shape[0], tiles.shape[1]
    per = dst_blocks // owners
    return pl.pallas_call(
        aggregate_kernel,
        grid_spec=pltpu.PrefetchScalarGridSpec(
            num_scalar_prefetch=3,
            grid=(owners,),
            in_specs=[
                pl.BlockSpec(memory_space=pltpu.VMEM),
                pl.BlockSpec(memory_space=pltpu.VMEM),
                pl.BlockSpec((per, slots, BLOCK, BLOCK), lambda r, *_: (r, 0, 0, 0)),
            ],
            out_specs=pl.BlockSpec((1, width, per * BLOCK), lambda r, *_: (r, 0, 0)),
            scratch_shapes=[pltpu.VMEM((blocks + 1, width + 16, BLOCK), jnp.bfloat16)],
        ),
        out_shape=jax.ShapeDtypeStruct((owners, width, per * BLOCK), jnp.bfloat16),
        compiler_params=pltpu.CompilerParams(vmem_limit_bytes=32 * MIB),
        cost_estimate=pl.CostEstimate(flops=4_000_000_000, bytes_accessed=20 * MIB, transcendentals=0),
        name="aggregate",
    )(which, lists, counts, ids, table, tiles)


def own_kernel(first_ref, ids_ref, moved_ref, weight_ref, bias_ref, own_ref, pre_ref):
    step = pl.program_id(0)
    per = own_ref.shape[1] // BLOCK
    for b in range(per):
        row = first_ref[0] + step * per + b
        within = jnp.bitwise_and(ids_ref[pl.ds(row, 1), :], BLOCK - 1)
        columns = slice(b * BLOCK, (b + 1) * BLOCK)
        own_ref[:, columns] = dot(moved_ref[:, columns], selector(within)).astype(jnp.bfloat16)
    pre_ref[...] = dot(weight_ref[...], own_ref[...]) + bias_ref[...]


def own_part(first, ids, moved, weight, bias):
    features, owned = moved.shape
    hidden = weight.shape[0]
    wide = 2 * BLOCK
    return pl.pallas_call(
        own_kernel,
        grid=(owned // wide,),
        in_specs=[
            pl.BlockSpec(memory_space=pltpu.SMEM),
            pl.BlockSpec(memory_space=pltpu.VMEM),
            pl.BlockSpec((features, wide), lambda i: (0, i)),
            pl.BlockSpec(memory_space=pltpu.VMEM),
            pl.BlockSpec(memory_space=pltpu.VMEM),
        ],
        out_specs=[
            pl.BlockSpec((features, wide), lambda i: (0, i)),
            pl.BlockSpec((hidden, wide), lambda i: (0, i)),
        ],
        out_shape=[
            jax.ShapeDtypeStruct((features, owned), jnp.bfloat16),
            jax.ShapeDtypeStruct((hidden, owned), jnp.float32),
        ],
        compiler_params=pltpu.CompilerParams(vmem_limit_bytes=24 * MIB),
        cost_estimate=pl.CostEstimate(flops=2_000_000_000, bytes_accessed=6 * MIB, transcendentals=0),
        name="own_part",
    )(first, ids, moved, weight, bias)


def gelu_and_slope(pre):
    c, k = 0.7978845608028654, 0.044715
    square = pre * pre
    t = jnp.tanh(c * pre * (1.0 + k * square))
    half = 0.5 * (1.0 + t)
    slope = half + 0.5 * pre * (1.0 - t * t) * (c * (1.0 + 3.0 * k * square))
    return pre * half, slope


def finish_kernel(
    place_ref, pre_ref, agg_ref, own_ref, weight_ref, upstream_ref, hidden_ref, keep_ref, send_ref, slope
):
    owned = pre_ref.shape[1]
    wide = 2 * BLOCK
    limit, core = place_ref[0], place_ref[1]
    for j in range(owned // wide):
        columns = slice(j * wide, (j + 1) * wide)
        pre = pre_ref[:, columns] + dot(weight_ref[...], agg_ref[:, columns])
        active, back = gelu_and_slope(pre)
        positions = j * wide + lax.broadcasted_iota(jnp.int32, (1, wide), 1)
        valid = jnp.where(positions < limit, 1.0, 0.0)
        hidden_ref[:, columns] = (active * valid).astype(jnp.bfloat16)
        slope[:, columns] = (upstream_ref[:, columns].astype(jnp.float32) * back * valid).astype(jnp.bfloat16)

    owners, share, _ = keep_ref.shape

    def grads(left_ref, out_ref):
        group = 4

        def part(i, carry):
            left = left_ref[pl.ds(pl.multiple_of(i * group * share, group * share), group * share), :]
            out_ref[pl.ds(i * group, group)] = dot(left, slope[...], NT).reshape(group, share, -1)
            return carry

        lax.fori_loop(0, owners // group, part, 0)

    @pl.when(core == 0)
    def _():
        grads(own_ref, keep_ref)
        grads(agg_ref, send_ref)

    @pl.when(core != 0)
    def _():
        grads(own_ref, send_ref)
        grads(agg_ref, keep_ref)


def finish(place, pre, agg, own, weight, upstream, owners):
    hidden, owned = pre.shape
    features = agg.shape[0]
    part = jax.ShapeDtypeStruct((owners, features // owners, hidden), jnp.float32)
    vmem = pl.BlockSpec(memory_space=pltpu.VMEM)
    return pl.pallas_call(
        finish_kernel,
        in_specs=[pl.BlockSpec(memory_space=pltpu.SMEM)] + [vmem] * 5,
        out_specs=[vmem] * 3,
        out_shape=[jax.ShapeDtypeStruct((hidden, owned), jnp.bfloat16), part, part],
        scratch_shapes=[pltpu.VMEM((hidden, owned), jnp.bfloat16)],
        compiler_params=pltpu.CompilerParams(vmem_limit_bytes=32 * MIB),
        cost_estimate=pl.CostEstimate(flops=2_000_000_000, bytes_accessed=9 * MIB, transcendentals=262144),
        name="finish",
    )(place, pre, agg, own, weight, upstream)


def on_device(
    node_table, node_ids, block_lists, block_counts, tiles, batch_sizes, w_self, w_neigh, bias, cotangent
):
    owners = lax.axis_size(FEAT)
    rank, core = lax.axis_index(FEAT), lax.axis_index("core")
    table = jnp.swapaxes(node_table[0], 0, 1)
    width = table.shape[0]
    ids = node_ids[0].reshape(-1, BLOCK)
    which = lax.shift_right_logical(ids[:, 0], 7)
    owned = cotangent.shape[1]

    mine = pick(which, table, owners)
    moved = lax.all_to_all(mine, FEAT, split_axis=0, concat_axis=0, tiled=True)
    aggregated = aggregate(which, block_lists[0].reshape(-1), block_counts[0], ids, table, tiles[0], owners)
    agg = lax.all_to_all(aggregated, FEAT, split_axis=0, concat_axis=0, tiled=True).reshape(-1, owned)

    first = (rank * (owned // BLOCK)).reshape(1)
    own, pre = own_part(first, ids, moved.reshape(-1, owned), w_self.T, bias[:, None])
    place = jnp.stack([batch_sizes[0] - rank * owned, core])
    hidden, keep, send = finish(place, pre, agg, own, w_neigh.T, cotangent[0].T, owners)

    got = lax.ppermute(send, "core", [(0, 1), (1, 0)])
    parts = lax.all_to_all(keep + got, FEAT, split_axis=0, concat_axis=0, tiled=True)
    total = jnp.sum(parts, axis=0)
    others = [lax.ppermute(total, "x", [(i, i ^ k) for i in range(4)]) for k in (1, 2, 3)]
    total = (total + others[0]) + (others[1] + others[2])
    other = lax.ppermute(total, "core", [(0, 1), (1, 0)])
    first_core = core == 0
    return (
        hidden.T[None],
        jnp.where(first_core, total, other),
        jnp.where(first_core, other, total),
    )


def solution(mesh):
    axes = Mesh(mesh.devices.reshape(4, 4, 4, 2), ("z", "y", "x", "core"))
    in_specs = (
        P(GRP, None, FEAT),
        P(GRP, None),
        P(GRP, None, None),
        P(GRP, None),
        P(GRP, None, None, None, None),
        P(GRP),
        P(),
        P(),
        P(),
        P(GRP, FEAT, None),
    )
    out_specs = (P(GRP, FEAT, None), P(FEAT, None), P(FEAT, None))
    return jax.shard_map(on_device, mesh=axes, in_specs=in_specs, out_specs=out_specs, check_vma=False)
```

```python
import jax
import jax.numpy as jnp
from jax import lax
from jax.experimental import pallas as pl
from jax.experimental.pallas import tpu as pltpu
from jax.sharding import Mesh, PartitionSpec as P

BLOCK = 128
MIB = 1 << 20
WHOLE = 60 * MIB
FEAT = ("z", "y")
GRP = ("x", "core")
NT = (((1,), (1,)), ((), ()))
NN = (((1,), (0,)), ((), ()))


def dot(left, right, dims=NN):
    return lax.dot_general(left, right, dims, preferred_element_type=jnp.float32)


def selector(within):
    rows = lax.broadcasted_iota(jnp.int32, (BLOCK, BLOCK), 0)
    return jnp.where(rows == within, 1.0, 0.0).astype(jnp.bfloat16)


def pick_kernel(which_ref, table_ref, out_ref, sem):
    owners, _, owned = out_ref.shape
    per = owned // BLOCK

    def start(b, carry):
        w = which_ref[b]
        pltpu.make_async_copy(
            table_ref.at[:, pl.ds(pl.multiple_of(w * BLOCK, BLOCK), BLOCK)],
            out_ref.at[b // per, :, pl.ds(pl.multiple_of((b % per) * BLOCK, BLOCK), BLOCK)],
            sem,
        ).start()
        return carry

    lax.fori_loop(0, owners * per, start, 0, unroll=8)
    pltpu.make_async_copy(out_ref, out_ref, sem).wait()


def pick(which, table, owners):
    width, rows = table.shape
    owned = rows // 2 // owners
    return pl.pallas_call(
        pick_kernel,
        out_shape=jax.ShapeDtypeStruct((owners, width, owned), table.dtype),
        in_specs=[pl.BlockSpec(memory_space=pltpu.SMEM), pl.BlockSpec(memory_space=pl.ANY)],
        out_specs=pl.BlockSpec(memory_space=pltpu.VMEM),
        scratch_shapes=[pltpu.SemaphoreType.DMA],
        compiler_params=pltpu.CompilerParams(vmem_limit_bytes=WHOLE),
        cost_estimate=pl.CostEstimate(flops=0, bytes_accessed=4 * MIB, transcendentals=0),
        name="pick_own_blocks",
    )(which, table)


def aggregate_kernel(
    which_ref, lists_ref, counts_ref, ids_ref, table_hbm, tiles_hbm, out_ref, source, table, tiles, sems
):
    blocks = ids_ref.shape[0]
    width = table.shape[0]
    owners = out_ref.shape[0]
    dst_blocks, slots = tiles.shape[0], tiles.shape[1]
    per = dst_blocks // owners

    def load_tiles(r):
        part = pl.ds(r * per, per)
        return pltpu.make_async_copy(tiles_hbm.at[part], tiles.at[part], sems.at[r])

    load_table = pltpu.make_async_copy(table_hbm, table, sems.at[owners])
    load_table.start()
    for r in range(owners):
        load_tiles(r).start()
    source[blocks] = jnp.zeros(source.shape[1:], source.dtype)
    load_table.wait()

    def place(n, carry):
        w = which_ref[n]
        chosen = table[:, pl.ds(pl.multiple_of(w * BLOCK, BLOCK), BLOCK)].astype(jnp.float32)
        within = jnp.broadcast_to(ids_ref[pl.ds(n, 1), :] - w * BLOCK, (8, BLOCK))
        rows = [jnp.take_along_axis(chosen[i : i + 8], within, axis=1) for i in range(0, width, 8)]
        source[n, :width] = jnp.concatenate(rows, axis=0).astype(jnp.bfloat16)
        source[n, width:] = jnp.ones((source.shape[1] - width, BLOCK), jnp.bfloat16)
        return carry

    lax.fori_loop(0, blocks, place, 0, unroll=16)

    def owner(r, carry):
        load_tiles(r).wait()
        for b in range(per):
            d = r * per + b
            count = counts_ref[d]
            used = [jnp.where(s < count, lists_ref[s * dst_blocks + d], blocks) for s in range(slots)]
            left = jnp.concatenate([source[u] for u in used], axis=1)
            right = jnp.concatenate([tiles[d, s] for s in range(slots)], axis=1)
            total = dot(left, right, NT)
            out_ref[r, :, b * BLOCK : (b + 1) * BLOCK] = (total[:width] / total[width : width + 1]).astype(
                jnp.bfloat16
            )
        return carry

    lax.fori_loop(0, owners, owner, 0)


def aggregate(which, lists, counts, ids, table, tiles, owners):
    width, rows = table.shape
    blocks = rows // BLOCK
    smem, vmem = pl.BlockSpec(memory_space=pltpu.SMEM), pl.BlockSpec(memory_space=pltpu.VMEM)
    anywhere = pl.BlockSpec(memory_space=pl.ANY)
    return pl.pallas_call(
        aggregate_kernel,
        in_specs=[smem, smem, smem, vmem, anywhere, anywhere],
        out_specs=vmem,
        out_shape=jax.ShapeDtypeStruct((owners, width, tiles.shape[0] // owners * BLOCK), jnp.bfloat16),
        scratch_shapes=[
            pltpu.VMEM((blocks + 1, width + 16, BLOCK), jnp.bfloat16),
            pltpu.VMEM(table.shape, jnp.bfloat16),
            pltpu.VMEM(tiles.shape, jnp.bfloat16),
            pltpu.SemaphoreType.DMA((owners + 1,)),
        ],
        compiler_params=pltpu.CompilerParams(vmem_limit_bytes=WHOLE),
        cost_estimate=pl.CostEstimate(flops=4_000_000_000, bytes_accessed=20 * MIB, transcendentals=0),
        name="aggregate",
    )(which, lists, counts, ids, table, tiles)


def own_kernel(first_ref, ids_ref, moved_ref, weight_ref, bias_ref, own_ref, pre_ref):
    step = pl.program_id(0)
    per = own_ref.shape[1] // BLOCK
    for b in range(per):
        row = first_ref[0] + step * per + b
        within = jnp.bitwise_and(ids_ref[pl.ds(row, 1), :], BLOCK - 1)
        columns = slice(b * BLOCK, (b + 1) * BLOCK)
        own_ref[:, columns] = dot(moved_ref[:, columns], selector(within)).astype(jnp.bfloat16)
    pre_ref[...] = dot(weight_ref[...], own_ref[...]) + bias_ref[...]


def own_part(first, ids, moved, weight, bias):
    features, owned = moved.shape
    hidden = weight.shape[0]
    wide = 2 * BLOCK
    return pl.pallas_call(
        own_kernel,
        grid=(owned // wide,),
        in_specs=[
            pl.BlockSpec(memory_space=pltpu.SMEM),
            pl.BlockSpec(memory_space=pltpu.VMEM),
            pl.BlockSpec((features, wide), lambda i: (0, i)),
            pl.BlockSpec(memory_space=pltpu.VMEM),
            pl.BlockSpec(memory_space=pltpu.VMEM),
        ],
        out_specs=[
            pl.BlockSpec((features, wide), lambda i: (0, i)),
            pl.BlockSpec((hidden, wide), lambda i: (0, i)),
        ],
        out_shape=[
            jax.ShapeDtypeStruct((features, owned), jnp.bfloat16),
            jax.ShapeDtypeStruct((hidden, owned), jnp.float32),
        ],
        compiler_params=pltpu.CompilerParams(vmem_limit_bytes=24 * MIB),
        cost_estimate=pl.CostEstimate(flops=2_000_000_000, bytes_accessed=6 * MIB, transcendentals=0),
        name="own_part",
    )(first, ids, moved, weight, bias)


def gelu_and_slope(pre):
    c, k = 0.7978845608028654, 0.044715
    square = pre * pre
    t = jnp.tanh(c * pre * (1.0 + k * square))
    half = 0.5 * (1.0 + t)
    slope = half + 0.5 * pre * (1.0 - t * t) * (c * (1.0 + 3.0 * k * square))
    return pre * half, slope


def finish_kernel(
    place_ref, pre_hbm, agg_hbm, own_hbm, weight_hbm, upstream_hbm, hidden_ref, keep_ref, send_ref,
    pre_ref, agg_ref, own_ref, weight_ref, upstream_ref, slope, sems,
):
    owned = pre_ref.shape[1]
    wide = 2 * BLOCK
    chunks = [slice(j, j + wide) for j in range(0, owned, wide)]
    limit, core = place_ref[0], place_ref[1]

    loads = [pltpu.make_async_copy(weight_hbm, weight_ref, sems.at[0])]
    for j, columns in enumerate(chunks):
        loads.append(pltpu.make_async_copy(agg_hbm.at[:, columns], agg_ref.at[:, columns], sems.at[j + 1]))
    loads.append(pltpu.make_async_copy(pre_hbm, pre_ref, sems.at[len(chunks) + 1]))
    loads.append(pltpu.make_async_copy(upstream_hbm, upstream_ref, sems.at[len(chunks) + 2]))
    loads.append(pltpu.make_async_copy(own_hbm, own_ref, sems.at[len(chunks) + 3]))
    for load in loads:
        load.start()
    loads[0].wait()

    for j, columns in enumerate(chunks):
        loads[j + 1].wait()
        pre = dot(weight_ref[...], agg_ref[:, columns])
        if j == 0:
            loads[-3].wait()
            loads[-2].wait()
        active, back = gelu_and_slope(pre + pre_ref[:, columns])
        positions = j * wide + lax.broadcasted_iota(jnp.int32, (1, wide), 1)
        valid = jnp.where(positions < limit, 1.0, 0.0)
        hidden_ref[:, columns] = (active * valid).astype(jnp.bfloat16)
        slope[:, columns] = (upstream_ref[:, columns].astype(jnp.float32) * back * valid).astype(jnp.bfloat16)
    loads[-1].wait()

    owners, share, _ = keep_ref.shape

    def grads(left_ref, out_ref):
        group = 4

        def part(i, carry):
            left = left_ref[pl.ds(pl.multiple_of(i * group * share, group * share), group * share), :]
            total = dot(left, slope[...], NT).reshape(group, share, -1)
            out_ref[pl.ds(i * group, group)] = total.astype(out_ref.dtype)
            return carry

        lax.fori_loop(0, owners // group, part, 0)

    @pl.when(core == 0)
    def _():
        grads(own_ref, keep_ref)
        grads(agg_ref, send_ref)

    @pl.when(core != 0)
    def _():
        grads(own_ref, send_ref)
        grads(agg_ref, keep_ref)


def finish(place, pre, agg, own, weight, upstream, owners):
    hidden, owned = pre.shape
    features = agg.shape[0]
    part = (owners, features // owners, hidden)
    vmem, anywhere = pl.BlockSpec(memory_space=pltpu.VMEM), pl.BlockSpec(memory_space=pl.ANY)
    return pl.pallas_call(
        finish_kernel,
        in_specs=[pl.BlockSpec(memory_space=pltpu.SMEM)] + [anywhere] * 5,
        out_specs=[vmem] * 3,
        out_shape=[
            jax.ShapeDtypeStruct((hidden, owned), jnp.bfloat16),
            jax.ShapeDtypeStruct(part, jnp.float32),
            jax.ShapeDtypeStruct(part, jnp.bfloat16),
        ],
        scratch_shapes=[pltpu.VMEM(a.shape, a.dtype) for a in (pre, agg, own, weight, upstream)]
        + [pltpu.VMEM((hidden, owned), jnp.bfloat16), pltpu.SemaphoreType.DMA((owned // (2 * BLOCK) + 4,))],
        compiler_params=pltpu.CompilerParams(vmem_limit_bytes=WHOLE),
        cost_estimate=pl.CostEstimate(flops=2_000_000_000, bytes_accessed=9 * MIB, transcendentals=262144),
        name="finish",
    )(place, pre, agg, own, weight, upstream)


def on_device(
    node_table, node_ids, block_lists, block_counts, tiles, batch_sizes, w_self, w_neigh, bias, cotangent
):
    owners = lax.axis_size(FEAT)
    rank, core = lax.axis_index(FEAT), lax.axis_index("core")
    table = jnp.swapaxes(node_table[0], 0, 1)
    width = table.shape[0]
    ids = node_ids[0].reshape(-1, BLOCK)
    which = lax.shift_right_logical(ids[:, 0], 7)
    owned = cotangent.shape[1]

    mine = pick(which, table, owners)
    moved = lax.all_to_all(mine, FEAT, split_axis=0, concat_axis=0, tiled=True)
    aggregated = aggregate(which, block_lists[0].T.reshape(-1), block_counts[0], ids, table, tiles[0], owners)
    agg = lax.all_to_all(aggregated, FEAT, split_axis=0, concat_axis=0, tiled=True).reshape(-1, owned)

    first = (rank * (owned // BLOCK)).reshape(1)
    own, pre = own_part(first, ids, moved.reshape(-1, owned), w_self.T, bias[:, None])
    place = jnp.stack([batch_sizes[0] - rank * owned, core])
    hidden, keep, send = finish(place, pre, agg, own, w_neigh.T, cotangent[0].T, owners)

    got = lax.ppermute(send, "core", [(0, 1), (1, 0)])
    parts = lax.all_to_all((keep + got).astype(jnp.bfloat16), FEAT, split_axis=0, concat_axis=0, tiled=True)
    total = jnp.sum(parts, axis=0, dtype=jnp.float32)
    others = [lax.ppermute(total, "x", [(i, i ^ k) for i in range(4)]) for k in (1, 2, 3)]
    total = (total + others[0]) + (others[1] + others[2])
    other = lax.ppermute(total, "core", [(0, 1), (1, 0)])
    first_core = core == 0
    return (
        hidden.T[None],
        jnp.where(first_core, total, other),
        jnp.where(first_core, other, total),
    )


def solution(mesh):
    axes = Mesh(mesh.devices.reshape(4, 4, 4, 2), ("z", "y", "x", "core"))
    in_specs = (
        P(GRP, None, FEAT),
        P(GRP, None),
        P(GRP, None, None),
        P(GRP, None),
        P(GRP, None, None, None, None),
        P(GRP),
        P(),
        P(),
        P(),
        P(GRP, FEAT, None),
    )
    out_specs = (P(GRP, FEAT, None), P(FEAT, None), P(FEAT, None))
    return jax.shard_map(on_device, mesh=axes, in_specs=in_specs, out_specs=out_specs, check_vma=False)
```

```python
import jax
import jax.numpy as jnp
from jax import lax
from jax.experimental import pallas as pl
from jax.experimental.pallas import tpu as pltpu
from jax.sharding import Mesh, PartitionSpec as P

BLOCK = 128
MIB = 1 << 20
WHOLE = 60 * MIB
FEAT = ("z", "y")
GRP = ("x", "core")
NT = (((1,), (1,)), ((), ()))
NN = (((1,), (0,)), ((), ()))


def dot(left, right, dims=NN):
    return lax.dot_general(left, right, dims, preferred_element_type=jnp.float32)


def selector(within):
    rows = lax.broadcasted_iota(jnp.int32, (BLOCK, BLOCK), 0)
    return jnp.where(rows == within, 1.0, 0.0).astype(jnp.bfloat16)


def place_blocks(which_ref, ids_ref, table, source):
    width = table.shape[0]

    def place(n, carry):
        w = which_ref[n]
        chosen = table[:, pl.ds(pl.multiple_of(w * BLOCK, BLOCK), BLOCK)].astype(jnp.float32)
        within = jnp.broadcast_to(ids_ref[pl.ds(n, 1), :] - w * BLOCK, (8, BLOCK))
        rows = [jnp.take_along_axis(chosen[i : i + 8], within, axis=1) for i in range(0, width, 8)]
        source[n, :width] = jnp.concatenate(rows, axis=0).astype(jnp.bfloat16)
        return carry

    lax.fori_loop(0, ids_ref.shape[0], place, 0, unroll=16)


def pick_kernel(core_ref, which_ref, ids_ref, table_hbm, out_ref, placed_hbm, table, placed, sems):
    owners, _, owned = out_ref.shape
    per = owned // BLOCK

    def start(b, carry):
        w = which_ref[b]
        pltpu.make_async_copy(
            table_hbm.at[:, pl.ds(pl.multiple_of(w * BLOCK, BLOCK), BLOCK)],
            out_ref.at[b // per, :, pl.ds(pl.multiple_of((b % per) * BLOCK, BLOCK), BLOCK)],
            sems.at[0],
        ).start()
        return carry

    lax.fori_loop(0, owners * per, start, 0, unroll=8)

    @pl.when(core_ref[0] == 1)
    def _():
        load = pltpu.make_async_copy(table_hbm, table, sems.at[1])
        load.start()
        load.wait()
        place_blocks(which_ref, ids_ref, table, placed)
        store = pltpu.make_async_copy(placed, placed_hbm, sems.at[2])
        store.start()
        store.wait()

    pltpu.make_async_copy(out_ref, out_ref, sems.at[0]).wait()


def pick(core, which, ids, table, owners):
    width, rows = table.shape
    owned = rows // 2 // owners
    placed = (rows // BLOCK, width, BLOCK)
    smem, vmem = pl.BlockSpec(memory_space=pltpu.SMEM), pl.BlockSpec(memory_space=pltpu.VMEM)
    anywhere = pl.BlockSpec(memory_space=pl.ANY)
    return pl.pallas_call(
        pick_kernel,
        out_shape=[
            jax.ShapeDtypeStruct((owners, width, owned), table.dtype),
            jax.ShapeDtypeStruct(placed, table.dtype),
        ],
        in_specs=[smem, smem, vmem, anywhere],
        out_specs=[vmem, anywhere],
        scratch_shapes=[
            pltpu.VMEM(table.shape, table.dtype),
            pltpu.VMEM(placed, table.dtype),
            pltpu.SemaphoreType.DMA((3,)),
        ],
        compiler_params=pltpu.CompilerParams(vmem_limit_bytes=WHOLE),
        cost_estimate=pl.CostEstimate(flops=0, bytes_accessed=4 * MIB, transcendentals=0),
        name="pick_own_blocks",
    )(core, which, ids, table)


def aggregate_kernel(
    core_ref, which_ref, lists_ref, counts_ref, ids_ref, table_hbm, placed_hbm, tiles_hbm, out_ref,
    source, table, tiles, sems,
):
    blocks = ids_ref.shape[0]
    width = table.shape[0]
    owners = out_ref.shape[0]
    dst_blocks, slots = tiles.shape[0], tiles.shape[1]
    per = dst_blocks // owners
    core = core_ref[0]

    def load_tiles(r):
        part = pl.ds(r * per, per)
        return pltpu.make_async_copy(tiles_hbm.at[part], tiles.at[part], sems.at[r])

    load_table = pltpu.make_async_copy(table_hbm, table, sems.at[owners])
    load_placed = pltpu.make_async_copy(placed_hbm, source.at[pl.ds(0, blocks), pl.ds(0, width)], sems.at[owners])

    @pl.when(core == 0)
    def _():
        load_table.start()

    @pl.when(core == 1)
    def _():
        load_placed.start()

    for r in range(owners):
        load_tiles(r).start()
    source[:blocks, width:] = jnp.ones((blocks, source.shape[1] - width, BLOCK), source.dtype)
    source[blocks] = jnp.zeros(source.shape[1:], source.dtype)

    @pl.when(core == 0)
    def _():
        load_table.wait()
        place_blocks(which_ref, ids_ref, table, source)

    @pl.when(core == 1)
    def _():
        load_placed.wait()

    def owner(r, carry):
        load_tiles(r).wait()
        for b in range(per):
            d = r * per + b
            count = counts_ref[d]
            used = [jnp.where(s < count, lists_ref[s * dst_blocks + d], blocks) for s in range(slots)]
            left = jnp.concatenate([source[u] for u in used], axis=1)
            right = jnp.concatenate([tiles[d, s] for s in range(slots)], axis=1)
            total = dot(left, right, NT)
            out_ref[r, :, b * BLOCK : (b + 1) * BLOCK] = (total[:width] / total[width : width + 1]).astype(
                jnp.bfloat16
            )
        return carry

    lax.fori_loop(0, owners, owner, 0)


def aggregate(core, which, lists, counts, ids, table, placed, tiles, owners):
    width, rows = table.shape
    blocks = rows // BLOCK
    smem, vmem = pl.BlockSpec(memory_space=pltpu.SMEM), pl.BlockSpec(memory_space=pltpu.VMEM)
    anywhere = pl.BlockSpec(memory_space=pl.ANY)
    return pl.pallas_call(
        aggregate_kernel,
        in_specs=[smem, smem, smem, smem, vmem, anywhere, anywhere, anywhere],
        out_specs=vmem,
        out_shape=jax.ShapeDtypeStruct((owners, width, tiles.shape[0] // owners * BLOCK), jnp.bfloat16),
        scratch_shapes=[
            pltpu.VMEM((blocks + 1, width + 16, BLOCK), jnp.bfloat16),
            pltpu.VMEM(table.shape, jnp.bfloat16),
            pltpu.VMEM(tiles.shape, jnp.bfloat16),
            pltpu.SemaphoreType.DMA((owners + 1,)),
        ],
        compiler_params=pltpu.CompilerParams(vmem_limit_bytes=WHOLE),
        cost_estimate=pl.CostEstimate(flops=4_000_000_000, bytes_accessed=20 * MIB, transcendentals=0),
        name="aggregate",
    )(core, which, lists, counts, ids, table, placed, tiles)


def own_kernel(first_ref, ids_ref, moved_ref, weight_ref, bias_ref, own_ref, pre_ref):
    step = pl.program_id(0)
    per = own_ref.shape[1] // BLOCK
    for b in range(per):
        row = first_ref[0] + step * per + b
        within = jnp.bitwise_and(ids_ref[pl.ds(row, 1), :], BLOCK - 1)
        columns = slice(b * BLOCK, (b + 1) * BLOCK)
        own_ref[:, columns] = dot(moved_ref[:, columns], selector(within)).astype(jnp.bfloat16)
    pre_ref[...] = dot(weight_ref[...], own_ref[...]) + bias_ref[...]


def own_part(first, ids, moved, weight, bias):
    features, owned = moved.shape
    hidden = weight.shape[0]
    wide = 2 * BLOCK
    return pl.pallas_call(
        own_kernel,
        grid=(owned // wide,),
        in_specs=[
            pl.BlockSpec(memory_space=pltpu.SMEM),
            pl.BlockSpec(memory_space=pltpu.VMEM),
            pl.BlockSpec((features, wide), lambda i: (0, i)),
            pl.BlockSpec(memory_space=pltpu.VMEM),
            pl.BlockSpec(memory_space=pltpu.VMEM),
        ],
        out_specs=[
            pl.BlockSpec((features, wide), lambda i: (0, i)),
            pl.BlockSpec((hidden, wide), lambda i: (0, i)),
        ],
        out_shape=[
            jax.ShapeDtypeStruct((features, owned), jnp.bfloat16),
            jax.ShapeDtypeStruct((hidden, owned), jnp.float32),
        ],
        compiler_params=pltpu.CompilerParams(vmem_limit_bytes=24 * MIB),
        cost_estimate=pl.CostEstimate(flops=2_000_000_000, bytes_accessed=6 * MIB, transcendentals=0),
        name="own_part",
    )(first, ids, moved, weight, bias)


def gelu_and_slope(pre):
    c, k = 0.7978845608028654, 0.044715
    square = pre * pre
    t = jnp.tanh(c * pre * (1.0 + k * square))
    half = 0.5 * (1.0 + t)
    slope = half + 0.5 * pre * (1.0 - t * t) * (c * (1.0 + 3.0 * k * square))
    return pre * half, slope


def finish_kernel(
    place_ref, pre_hbm, agg_hbm, own_hbm, weight_hbm, upstream_hbm, hidden_ref, keep_ref, send_ref,
    pre_ref, agg_ref, own_ref, weight_ref, upstream_ref, slope, sems,
):
    owned = pre_ref.shape[1]
    wide = 2 * BLOCK
    chunks = [slice(j, j + wide) for j in range(0, owned, wide)]
    limit, core = place_ref[0], place_ref[1]

    loads = [pltpu.make_async_copy(weight_hbm, weight_ref, sems.at[0])]
    for j, columns in enumerate(chunks):
        loads.append(pltpu.make_async_copy(agg_hbm.at[:, columns], agg_ref.at[:, columns], sems.at[j + 1]))
    loads.append(pltpu.make_async_copy(pre_hbm, pre_ref, sems.at[len(chunks) + 1]))
    loads.append(pltpu.make_async_copy(upstream_hbm, upstream_ref, sems.at[len(chunks) + 2]))
    loads.append(pltpu.make_async_copy(own_hbm, own_ref, sems.at[len(chunks) + 3]))
    for load in loads:
        load.start()
    loads[0].wait()

    for j, columns in enumerate(chunks):
        loads[j + 1].wait()
        pre = dot(weight_ref[...], agg_ref[:, columns])
        if j == 0:
            loads[-3].wait()
            loads[-2].wait()
        active, back = gelu_and_slope(pre + pre_ref[:, columns])
        positions = j * wide + lax.broadcasted_iota(jnp.int32, (1, wide), 1)
        valid = jnp.where(positions < limit, 1.0, 0.0)
        hidden_ref[:, columns] = (active * valid).astype(jnp.bfloat16)
        slope[:, columns] = (upstream_ref[:, columns].astype(jnp.float32) * back * valid).astype(jnp.bfloat16)
    loads[-1].wait()

    owners, share, _ = keep_ref.shape

    def grads(left_ref, out_ref):
        group = 4

        def part(i, carry):
            left = left_ref[pl.ds(pl.multiple_of(i * group * share, group * share), group * share), :]
            total = dot(left, slope[...], NT).reshape(group, share, -1)
            out_ref[pl.ds(i * group, group)] = total.astype(out_ref.dtype)
            return carry

        lax.fori_loop(0, owners // group, part, 0)

    @pl.when(core == 0)
    def _():
        grads(own_ref, keep_ref)
        grads(agg_ref, send_ref)

    @pl.when(core != 0)
    def _():
        grads(own_ref, send_ref)
        grads(agg_ref, keep_ref)


def finish(place, pre, agg, own, weight, upstream, owners):
    hidden, owned = pre.shape
    features = agg.shape[0]
    part = (owners, features // owners, hidden)
    vmem, anywhere = pl.BlockSpec(memory_space=pltpu.VMEM), pl.BlockSpec(memory_space=pl.ANY)
    return pl.pallas_call(
        finish_kernel,
        in_specs=[pl.BlockSpec(memory_space=pltpu.SMEM)] + [anywhere] * 5,
        out_specs=[vmem] * 3,
        out_shape=[
            jax.ShapeDtypeStruct((hidden, owned), jnp.bfloat16),
            jax.ShapeDtypeStruct(part, jnp.float32),
            jax.ShapeDtypeStruct(part, jnp.bfloat16),
        ],
        scratch_shapes=[pltpu.VMEM(a.shape, a.dtype) for a in (pre, agg, own, weight, upstream)]
        + [pltpu.VMEM((hidden, owned), jnp.bfloat16), pltpu.SemaphoreType.DMA((owned // (2 * BLOCK) + 4,))],
        compiler_params=pltpu.CompilerParams(vmem_limit_bytes=WHOLE),
        cost_estimate=pl.CostEstimate(flops=2_000_000_000, bytes_accessed=9 * MIB, transcendentals=262144),
        name="finish",
    )(place, pre, agg, own, weight, upstream)


def on_device(
    node_table, node_ids, block_lists, block_counts, tiles, batch_sizes, w_self, w_neigh, bias, cotangent
):
    owners = lax.axis_size(FEAT)
    rank, core = lax.axis_index(FEAT), lax.axis_index("core")
    table = jnp.swapaxes(node_table[0], 0, 1)
    width = table.shape[0]
    ids = node_ids[0].reshape(-1, BLOCK)
    which = lax.shift_right_logical(ids[:, 0], 7)
    owned = cotangent.shape[1]

    mine, placed = pick(core.reshape(1), which, ids, table, owners)
    moved = lax.all_to_all(mine, FEAT, split_axis=0, concat_axis=0, tiled=True)
    lists = block_lists[0].T.reshape(-1)
    aggregated = aggregate(
        core.reshape(1), which, lists, block_counts[0], ids, table, placed, tiles[0], owners
    )
    agg = lax.all_to_all(aggregated, FEAT, split_axis=0, concat_axis=0, tiled=True).reshape(-1, owned)

    first = (rank * (owned // BLOCK)).reshape(1)
    own, pre = own_part(first, ids, moved.reshape(-1, owned), w_self.T, bias[:, None])
    place = jnp.stack([batch_sizes[0] - rank * owned, core])
    hidden, keep, send = finish(place, pre, agg, own, w_neigh.T, cotangent[0].T, owners)

    got = lax.ppermute(send, "core", [(0, 1), (1, 0)])
    parts = lax.all_to_all((keep + got).astype(jnp.bfloat16), FEAT, split_axis=0, concat_axis=0, tiled=True)
    total = jnp.sum(parts, axis=0, dtype=jnp.float32)
    others = [lax.ppermute(total, "x", [(i, i ^ k) for i in range(4)]) for k in (1, 2, 3)]
    total = (total + others[0]) + (others[1] + others[2])
    other = lax.ppermute(total, "core", [(0, 1), (1, 0)])
    first_core = core == 0
    return (
        hidden.T[None],
        jnp.where(first_core, total, other),
        jnp.where(first_core, other, total),
    )


def solution(mesh):
    axes = Mesh(mesh.devices.reshape(4, 4, 4, 2), ("z", "y", "x", "core"))
    in_specs = (
        P(GRP, None, FEAT),
        P(GRP, None),
        P(GRP, None, None),
        P(GRP, None),
        P(GRP, None, None, None, None),
        P(GRP),
        P(),
        P(),
        P(),
        P(GRP, FEAT, None),
    )
    out_specs = (P(GRP, FEAT, None), P(FEAT, None), P(FEAT, None))
    return jax.shard_map(on_device, mesh=axes, in_specs=in_specs, out_specs=out_specs, check_vma=False)
```

```python
import jax
import jax.numpy as jnp
from jax import lax
from jax.experimental import pallas as pl
from jax.experimental.pallas import tpu as pltpu
from jax.sharding import Mesh, PartitionSpec as P

BLOCK = 128
MIB = 1 << 20
WHOLE = 60 * MIB
FEAT = ("z", "y")
GRP = ("x", "core")
NT = (((1,), (1,)), ((), ()))
NN = (((1,), (0,)), ((), ()))


def dot(left, right, dims=NN):
    return lax.dot_general(left, right, dims, preferred_element_type=jnp.float32)


def selector(within):
    rows = lax.broadcasted_iota(jnp.int32, (BLOCK, BLOCK), 0)
    return jnp.where(rows == within, 1.0, 0.0).astype(jnp.bfloat16)


def place_blocks(which_ref, ids_ref, table, count, store):
    width = table.shape[0]

    def place(n, carry):
        w = which_ref[n]
        chosen = table[:, pl.ds(pl.multiple_of(w * BLOCK, BLOCK), BLOCK)].astype(jnp.float32)
        within = jnp.broadcast_to(ids_ref[pl.ds(n, 1), :] - w * BLOCK, (8, BLOCK))
        rows = [jnp.take_along_axis(chosen[i : i + 8], within, axis=1) for i in range(0, width, 8)]
        store(n, jnp.concatenate(rows, axis=0).astype(jnp.bfloat16))
        return carry

    lax.fori_loop(0, count, place, 0, unroll=16)


def pick_blocks(which_ref, table_hbm, out_ref, sem):
    owners, _, owned = out_ref.shape
    per = owned // BLOCK

    def start(b, carry):
        w = which_ref[b]
        pltpu.make_async_copy(
            table_hbm.at[:, pl.ds(pl.multiple_of(w * BLOCK, BLOCK), BLOCK)],
            out_ref.at[b // per, :, pl.ds(pl.multiple_of((b % per) * BLOCK, BLOCK), BLOCK)],
            sem,
        ).start()
        return carry

    lax.fori_loop(0, owners * per, start, 0, unroll=8)
    pltpu.make_async_copy(out_ref, out_ref, sem).wait()


def aggregate_blocks(
    which_ref, lists_ref, counts_ref, ids_ref, table_hbm, tiles_hbm, out_ref, source, table, tiles, sems
):
    blocks = ids_ref.shape[0]
    width = table.shape[0]
    owners = out_ref.shape[0]
    dst_blocks, slots = tiles.shape[0], tiles.shape[1]
    per = dst_blocks // owners

    def load_tiles(r):
        part = pl.ds(r * per, per)
        return pltpu.make_async_copy(tiles_hbm.at[part], tiles.at[part], sems.at[r])

    load_table = pltpu.make_async_copy(table_hbm, table, sems.at[owners])
    load_table.start()
    for r in range(owners):
        load_tiles(r).start()
    source[:blocks, width:] = jnp.ones((blocks, source.shape[1] - width, BLOCK), source.dtype)
    source[blocks] = jnp.zeros(source.shape[1:], source.dtype)
    load_table.wait()

    def store(n, rows):
        source[n, :width] = rows

    place_blocks(which_ref, ids_ref, table, blocks, store)

    def owner(r, carry):
        load_tiles(r).wait()
        for b in range(per):
            d = r * per + b
            count = counts_ref[d]
            used = [jnp.where(s < count, lists_ref[s * dst_blocks + d], blocks) for s in range(slots)]
            left = jnp.concatenate([source[u] for u in used], axis=1)
            right = jnp.concatenate([tiles[d, s] for s in range(slots)], axis=1)
            total = dot(left, right, NT)
            out_ref[r, :, b * BLOCK : (b + 1) * BLOCK] = (total[:width] / total[width : width + 1]).astype(
                jnp.bfloat16
            )
        return carry

    lax.fori_loop(0, owners, owner, 0)


def first_kernel(
    core_ref, which_ref, lists_ref, counts_ref, ids_ref, table_hbm, tiles_hbm, out_ref, source, table, tiles, sems
):
    @pl.when(core_ref[0] == 0)
    def _():
        pick_blocks(which_ref, table_hbm, out_ref, sems.at[0])

    @pl.when(core_ref[0] == 1)
    def _():
        aggregate_blocks(
            which_ref, lists_ref, counts_ref, ids_ref, table_hbm, tiles_hbm, out_ref, source, table, tiles, sems
        )


def second_kernel(
    core_ref, which_ref, lists_ref, counts_ref, ids_ref, table_hbm, tiles_hbm, out_ref, source, table, tiles, sems
):
    owners, _, owned = out_ref.shape
    per = owned // BLOCK

    @pl.when(core_ref[0] == 1)
    def _():
        load = pltpu.make_async_copy(table_hbm, table, sems.at[0])
        load.start()
        load.wait()

        def store(n, rows):
            out_ref[n // per, :, pl.ds(pl.multiple_of((n % per) * BLOCK, BLOCK), BLOCK)] = rows

        place_blocks(which_ref, ids_ref, table, owners * per, store)

    @pl.when(core_ref[0] == 0)
    def _():
        aggregate_blocks(
            which_ref, lists_ref, counts_ref, ids_ref, table_hbm, tiles_hbm, out_ref, source, table, tiles, sems
        )


def outgoing(kernel, core, which, lists, counts, ids, table, tiles, owners, name):
    width, rows = table.shape
    blocks = rows // BLOCK
    smem, vmem = pl.BlockSpec(memory_space=pltpu.SMEM), pl.BlockSpec(memory_space=pltpu.VMEM)
    anywhere = pl.BlockSpec(memory_space=pl.ANY)
    return pl.pallas_call(
        kernel,
        in_specs=[smem, smem, smem, smem, vmem, anywhere, anywhere],
        out_specs=vmem,
        out_shape=jax.ShapeDtypeStruct((owners, width, tiles.shape[0] // owners * BLOCK), jnp.bfloat16),
        scratch_shapes=[
            pltpu.VMEM((blocks + 1, width + 16, BLOCK), jnp.bfloat16),
            pltpu.VMEM(table.shape, jnp.bfloat16),
            pltpu.VMEM(tiles.shape, jnp.bfloat16),
            pltpu.SemaphoreType.DMA((owners + 1,)),
        ],
        compiler_params=pltpu.CompilerParams(vmem_limit_bytes=WHOLE),
        cost_estimate=pl.CostEstimate(flops=4_000_000_000, bytes_accessed=20 * MIB, transcendentals=0),
        name=name,
    )(core, which, lists, counts, ids, table, tiles)


def arrived_kernel(place_ref, ids_ref, moved_ref, weight_ref, bias_ref, rows_ref, pre_ref):
    step = pl.program_id(0)
    per = rows_ref.shape[1] // BLOCK
    in_order = lax.broadcasted_iota(jnp.int32, (1, BLOCK), 1)
    for b in range(per):
        row = place_ref[1] + step * per + b
        within = jnp.bitwise_and(ids_ref[pl.ds(row, 1), :], BLOCK - 1)
        within = jnp.where(place_ref[0] == 0, within, in_order)
        columns = slice(b * BLOCK, (b + 1) * BLOCK)
        rows_ref[:, columns] = dot(moved_ref[:, columns], selector(within)).astype(jnp.bfloat16)
    pre_ref[...] = dot(weight_ref[0], rows_ref[...]) + bias_ref[...]


def arrived(place, ids, moved, weights, bias):
    features, owned = moved.shape
    hidden = weights.shape[1]
    wide = 2 * BLOCK
    return pl.pallas_call(
        arrived_kernel,
        grid_spec=pltpu.PrefetchScalarGridSpec(
            num_scalar_prefetch=1,
            grid=(owned // wide,),
            in_specs=[
                pl.BlockSpec(memory_space=pltpu.VMEM),
                pl.BlockSpec((features, wide), lambda i, place: (0, i)),
                pl.BlockSpec((1, hidden, features), lambda i, place: (place[0], 0, 0)),
                pl.BlockSpec(memory_space=pltpu.VMEM),
            ],
            out_specs=[
                pl.BlockSpec((features, wide), lambda i, place: (0, i)),
                pl.BlockSpec((hidden, wide), lambda i, place: (0, i)),
            ],
        ),
        out_shape=[
            jax.ShapeDtypeStruct((features, owned), jnp.bfloat16),
            jax.ShapeDtypeStruct((hidden, owned), jnp.float32),
        ],
        compiler_params=pltpu.CompilerParams(vmem_limit_bytes=24 * MIB),
        cost_estimate=pl.CostEstimate(flops=2_000_000_000, bytes_accessed=6 * MIB, transcendentals=0),
        name="first_arrived",
    )(place, ids, moved, weights, bias)


def gelu_and_slope(pre):
    c, k = 0.7978845608028654, 0.044715
    square = pre * pre
    t = jnp.tanh(c * pre * (1.0 + k * square))
    half = 0.5 * (1.0 + t)
    slope = half + 0.5 * pre * (1.0 - t * t) * (c * (1.0 + 3.0 * k * square))
    return pre * half, slope


def finish_kernel(
    place_ref, pre_hbm, second_hbm, first_hbm, weights_hbm, upstream_hbm, hidden_ref, keep_ref, send_ref,
    pre_ref, second_ref, first_ref, weight_ref, upstream_ref, slope, sems,
):
    owned = pre_ref.shape[1]
    wide = 2 * BLOCK
    chunks = [slice(j, j + wide) for j in range(0, owned, wide)]
    core, limit = place_ref[0], place_ref[2]

    loads = [pltpu.make_async_copy(weights_hbm.at[1 - core], weight_ref, sems.at[0])]
    for j, columns in enumerate(chunks):
        loads.append(pltpu.make_async_copy(second_hbm.at[:, columns], second_ref.at[:, columns], sems.at[j + 1]))
    loads.append(pltpu.make_async_copy(pre_hbm, pre_ref, sems.at[len(chunks) + 1]))
    loads.append(pltpu.make_async_copy(upstream_hbm, upstream_ref, sems.at[len(chunks) + 2]))
    loads.append(pltpu.make_async_copy(first_hbm, first_ref, sems.at[len(chunks) + 3]))
    for load in loads:
        load.start()
    loads[0].wait()

    for j, columns in enumerate(chunks):
        loads[j + 1].wait()
        pre = dot(weight_ref[...], second_ref[:, columns])
        if j == 0:
            loads[-3].wait()
            loads[-2].wait()
        active, back = gelu_and_slope(pre + pre_ref[:, columns])
        positions = j * wide + lax.broadcasted_iota(jnp.int32, (1, wide), 1)
        valid = jnp.where(positions < limit, 1.0, 0.0)
        hidden_ref[:, columns] = (active * valid).astype(jnp.bfloat16)
        slope[:, columns] = (upstream_ref[:, columns].astype(jnp.float32) * back * valid).astype(jnp.bfloat16)
    loads[-1].wait()

    owners, share, _ = keep_ref.shape

    def grads(left_ref, out_ref):
        group = 4

        def part(i, carry):
            left = left_ref[pl.ds(pl.multiple_of(i * group * share, group * share), group * share), :]
            total = dot(left, slope[...], NT).reshape(group, share, -1)
            out_ref[pl.ds(i * group, group)] = total.astype(out_ref.dtype)
            return carry

        lax.fori_loop(0, owners // group, part, 0)

    grads(first_ref, keep_ref)
    grads(second_ref, send_ref)


def finish(place, pre, second, first, weights, upstream, owners):
    hidden, owned = pre.shape
    features = second.shape[0]
    part = (owners, features // owners, hidden)
    vmem, anywhere = pl.BlockSpec(memory_space=pltpu.VMEM), pl.BlockSpec(memory_space=pl.ANY)
    return pl.pallas_call(
        finish_kernel,
        in_specs=[pl.BlockSpec(memory_space=pltpu.SMEM)] + [anywhere] * 5,
        out_specs=[vmem] * 3,
        out_shape=[
            jax.ShapeDtypeStruct((hidden, owned), jnp.bfloat16),
            jax.ShapeDtypeStruct(part, jnp.float32),
            jax.ShapeDtypeStruct(part, jnp.bfloat16),
        ],
        scratch_shapes=[pltpu.VMEM(a.shape, a.dtype) for a in (pre, second, first, weights[0], upstream)]
        + [pltpu.VMEM((hidden, owned), jnp.bfloat16), pltpu.SemaphoreType.DMA((owned // (2 * BLOCK) + 4,))],
        compiler_params=pltpu.CompilerParams(vmem_limit_bytes=WHOLE),
        cost_estimate=pl.CostEstimate(flops=2_000_000_000, bytes_accessed=9 * MIB, transcendentals=262144),
        name="finish",
    )(place, pre, second, first, weights, upstream)


def on_device(
    node_table, node_ids, block_lists, block_counts, tiles, batch_sizes, w_self, w_neigh, bias, cotangent
):
    owners = lax.axis_size(FEAT)
    rank, core = lax.axis_index(FEAT), lax.axis_index("core")
    table = jnp.swapaxes(node_table[0], 0, 1)
    width = table.shape[0]
    ids = node_ids[0].reshape(-1, BLOCK)
    which = lax.shift_right_logical(ids[:, 0], 7)
    owned = cotangent.shape[1]

    lists = block_lists[0].T.reshape(-1)
    place = jnp.stack([core, rank * (owned // BLOCK), batch_sizes[0] - rank * owned])
    operands = (core.reshape(1), which, lists, block_counts[0], ids, table, tiles[0], owners)
    weights = jnp.stack([w_self.T, w_neigh.T])

    first = outgoing(first_kernel, *operands, "first_outgoing")
    moved = lax.all_to_all(first, FEAT, split_axis=0, concat_axis=0, tiled=True)
    second = outgoing(second_kernel, *operands, "second_outgoing")
    second = lax.all_to_all(second, FEAT, split_axis=0, concat_axis=0, tiled=True)
    first, pre = arrived(place, ids, moved.reshape(-1, owned), weights, bias[:, None])
    second = second.reshape(-1, owned)
    hidden, keep, send = finish(place, pre, second, first, weights, cotangent[0].T, owners)

    got = lax.ppermute(send, "core", [(0, 1), (1, 0)])
    parts = lax.all_to_all((keep + got).astype(jnp.bfloat16), FEAT, split_axis=0, concat_axis=0, tiled=True)
    total = jnp.sum(parts, axis=0, dtype=jnp.float32)
    others = [lax.ppermute(total, "x", [(i, i ^ k) for i in range(4)]) for k in (1, 2, 3)]
    total = (total + others[0]) + (others[1] + others[2])
    other = lax.ppermute(total, "core", [(0, 1), (1, 0)])
    first_core = core == 0
    return (
        hidden.T[None],
        jnp.where(first_core, total, other),
        jnp.where(first_core, other, total),
    )


def solution(mesh):
    axes = Mesh(mesh.devices.reshape(4, 4, 4, 2), ("z", "y", "x", "core"))
    in_specs = (
        P(GRP, None, FEAT),
        P(GRP, None),
        P(GRP, None, None),
        P(GRP, None),
        P(GRP, None, None, None, None),
        P(GRP),
        P(),
        P(),
        P(),
        P(GRP, FEAT, None),
    )
    out_specs = (P(GRP, FEAT, None), P(FEAT, None), P(FEAT, None))
    return jax.shard_map(on_device, mesh=axes, in_specs=in_specs, out_specs=out_specs, check_vma=False)
```

```python
import jax
import jax.numpy as jnp
from jax import lax
from jax.experimental import pallas as pl
from jax.experimental.pallas import tpu as pltpu
from jax.sharding import Mesh, PartitionSpec as P

BLOCK = 128
MIB = 1 << 20
WHOLE = 60 * MIB
FEAT = ("z", "y")
GRP = ("x", "core")
NT = (((1,), (1,)), ((), ()))
NN = (((1,), (0,)), ((), ()))


def dot(left, right, dims=NN):
    return lax.dot_general(left, right, dims, preferred_element_type=jnp.float32)


def selector(within):
    rows = lax.broadcasted_iota(jnp.int32, (BLOCK, BLOCK), 0)
    return jnp.where(rows == within, 1.0, 0.0).astype(jnp.bfloat16)


def read_blocks(ids_ref, vector, which, sem):
    lanes = lax.broadcasted_iota(jnp.int32, (vector.shape[0], BLOCK), 1)
    first = jnp.where(lanes == 0, 1.0, 0.0).astype(jnp.bfloat16)
    blocks = lax.shift_right_logical(ids_ref[...], 7).astype(jnp.float32).astype(jnp.bfloat16)
    vector[...] = dot(first, blocks, NT).astype(jnp.int32)
    copy = pltpu.make_async_copy(vector, which, sem)
    copy.start()
    copy.wait()


def block_of(table, w):
    return table[:, pl.ds(pl.multiple_of(w * BLOCK, BLOCK), BLOCK)]


def in_run_order(chosen, ids_row):
    within = jnp.broadcast_to(jnp.bitwise_and(ids_row, BLOCK - 1), (8, BLOCK))
    chosen = chosen.astype(jnp.float32)
    rows = [jnp.take_along_axis(chosen[i : i + 8], within, axis=1) for i in range(0, chosen.shape[0], 8)]
    return jnp.concatenate(rows, axis=0).astype(jnp.bfloat16)


def pick_blocks(ids_ref, table_hbm, out_hbm, rows, vector, which, load, leave):
    owners, _, owned = rows.shape
    per = owned // BLOCK
    read_blocks(ids_ref, vector, which, load.at[owners])

    def start(r, carry):
        for b in range(per):
            pltpu.make_async_copy(
                block_of(table_hbm.at, which[0, r * per + b]),
                rows.at[r, :, b * BLOCK : (b + 1) * BLOCK],
                load.at[r],
            ).start()
        return carry

    lax.fori_loop(0, owners, start, 0)
    for r in range(owners):
        pltpu.make_async_copy(rows.at[r], rows.at[r], load.at[r]).wait()
        pltpu.make_async_copy(rows.at[r], out_hbm.at[r], leave.at[r]).start()
    for r in range(owners):
        pltpu.make_async_copy(rows.at[r], out_hbm.at[r], leave.at[r]).wait()


def place_blocks(ids_ref, table_hbm, out_hbm, rows, table, vector, which, load, leave):
    owners, _, owned = rows.shape
    per = owned // BLOCK
    known = table.at[:, pl.ds(0, table_hbm.shape[1])]
    load_table = pltpu.make_async_copy(table_hbm, known, load.at[0])
    load_table.start()
    read_blocks(ids_ref, vector, which, load.at[owners])
    load_table.wait()

    def owner(r, carry):
        placed = []
        for b in range(per):
            n = r * per + b
            placed.append(in_run_order(block_of(table, which[0, n]), ids_ref[pl.ds(n, 1), :]))
        for b in range(per):
            rows[r, :, b * BLOCK : (b + 1) * BLOCK] = placed[b]
        pltpu.make_async_copy(rows.at[r], out_hbm.at[r], leave.at[r]).start()
        return carry

    lax.fori_loop(0, owners, owner, 0)
    for r in range(owners):
        pltpu.make_async_copy(rows.at[r], out_hbm.at[r], leave.at[r]).wait()


def aggregate_blocks(
    lists_ref, counts_ref, ids_ref, table_hbm, tiles_hbm, out_hbm, rows, table, tiles, vector, which, load, leave
):
    blocks = ids_ref.shape[0]
    owners, width, _ = rows.shape
    dst_blocks, slots = tiles.shape[0], tiles.shape[1]
    per = dst_blocks // owners
    together = 4

    def load_tiles(r):
        part = pl.ds(r * per, per)
        return pltpu.make_async_copy(tiles_hbm.at[part], tiles.at[part], load.at[r])

    known = table.at[:, pl.ds(0, table_hbm.shape[1])]
    load_table = pltpu.make_async_copy(table_hbm, known, load.at[owners + 1])
    load_table.start()
    for r in range(owners):
        load_tiles(r).start()
    table[:, table_hbm.shape[1] :] = jnp.zeros((width, BLOCK), table.dtype)
    read_blocks(ids_ref, vector, which, load.at[owners])
    load_table.wait()

    def one(d):
        count = counts_ref[0, d]
        left = []
        for s in range(slots):
            used = s < count
            n = lists_ref[s, 0, d]
            w = jnp.where(used, which[0, n], blocks)
            source = in_run_order(block_of(table, w), ids_ref[pl.ds(n, 1), :])
            ones = jnp.full((16, BLOCK), jnp.where(used, 1.0, 0.0), jnp.float32).astype(jnp.bfloat16)
            left.append(jnp.concatenate([source, ones], axis=0))
        right = jnp.concatenate([tiles[d, s] for s in range(slots)], axis=1)
        total = dot(jnp.concatenate(left, axis=1), right, NT)
        return (total[:width] * (1.0 / total[width : width + 1])).astype(jnp.bfloat16)

    def some(i, carry):
        for k in range(together):
            load_tiles(i * together + k).wait()
        results = [one(i * together * per + k) for k in range(together * per)]
        for k in range(together * per):
            rows[i * together + k // per, :, (k % per) * BLOCK : (k % per + 1) * BLOCK] = results[k]
        for k in range(together):
            r = i * together + k
            pltpu.make_async_copy(rows.at[r], out_hbm.at[r], leave.at[r]).start()
        return carry

    lax.fori_loop(0, owners // together, some, 0)
    for r in range(owners):
        pltpu.make_async_copy(rows.at[r], out_hbm.at[r], leave.at[r]).wait()


def first_kernel(
    core_ref, lists_ref, counts_ref, ids_ref, table_hbm, tiles_hbm, out_hbm,
    rows, table, tiles, vector, which, load, leave,
):
    @pl.when(core_ref[0] == 0)
    def _():
        pick_blocks(ids_ref, table_hbm, out_hbm, rows, vector, which, load, leave)

    @pl.when(core_ref[0] == 1)
    def _():
        aggregate_blocks(
            lists_ref, counts_ref, ids_ref, table_hbm, tiles_hbm, out_hbm,
            rows, table, tiles, vector, which, load, leave,
        )


def second_kernel(
    core_ref, lists_ref, counts_ref, ids_ref, table_hbm, tiles_hbm, out_hbm,
    rows, table, tiles, vector, which, load, leave,
):
    @pl.when(core_ref[0] == 1)
    def _():
        place_blocks(ids_ref, table_hbm, out_hbm, rows, table, vector, which, load, leave)

    @pl.when(core_ref[0] == 0)
    def _():
        aggregate_blocks(
            lists_ref, counts_ref, ids_ref, table_hbm, tiles_hbm, out_hbm,
            rows, table, tiles, vector, which, load, leave,
        )


def outgoing(kernel, core, lists, counts, ids, table, tiles, owners, name):
    width, rows = table.shape
    blocks = rows // BLOCK
    smem, vmem = pl.BlockSpec(memory_space=pltpu.SMEM), pl.BlockSpec(memory_space=pltpu.VMEM)
    anywhere = pl.BlockSpec(memory_space=pl.ANY)
    out = (owners, width, tiles.shape[0] // owners * BLOCK)
    return pl.pallas_call(
        kernel,
        in_specs=[smem, smem, smem, vmem, anywhere, anywhere],
        out_specs=anywhere,
        out_shape=jax.ShapeDtypeStruct(out, jnp.bfloat16),
        scratch_shapes=[
            pltpu.VMEM(out, jnp.bfloat16),
            pltpu.VMEM((width, rows + BLOCK), jnp.bfloat16),
            pltpu.VMEM(tiles.shape, jnp.bfloat16),
            pltpu.VMEM((8, blocks), jnp.int32),
            pltpu.SMEM((8, blocks), jnp.int32),
            pltpu.SemaphoreType.DMA((owners + 2,)),
            pltpu.SemaphoreType.DMA((owners,)),
        ],
        compiler_params=pltpu.CompilerParams(vmem_limit_bytes=WHOLE),
        cost_estimate=pl.CostEstimate(flops=4_000_000_000, bytes_accessed=20 * MIB, transcendentals=0),
        name=name,
    )(core, lists, counts, ids, table, tiles)


def arrived_kernel(place_ref, ids_ref, moved_ref, weight_ref, bias_ref, rows_ref, pre_ref):
    step = pl.program_id(0)
    per = rows_ref.shape[1] // BLOCK
    in_order = lax.broadcasted_iota(jnp.int32, (1, BLOCK), 1)
    for b in range(per):
        row = place_ref[1] + step * per + b
        within = jnp.bitwise_and(ids_ref[pl.ds(row, 1), :], BLOCK - 1)
        within = jnp.where(place_ref[0] == 0, within, in_order)
        columns = slice(b * BLOCK, (b + 1) * BLOCK)
        rows_ref[:, columns] = dot(moved_ref[:, columns], selector(within)).astype(jnp.bfloat16)
    pre_ref[...] = dot(weight_ref[0], rows_ref[...]) + bias_ref[...]


def arrived(place, ids, moved, weights, bias):
    features, owned = moved.shape
    hidden = weights.shape[1]
    wide = 2 * BLOCK
    return pl.pallas_call(
        arrived_kernel,
        grid_spec=pltpu.PrefetchScalarGridSpec(
            num_scalar_prefetch=1,
            grid=(owned // wide,),
            in_specs=[
                pl.BlockSpec(memory_space=pltpu.VMEM),
                pl.BlockSpec((features, wide), lambda i, place: (0, i)),
                pl.BlockSpec((1, hidden, features), lambda i, place: (place[0], 0, 0)),
                pl.BlockSpec(memory_space=pltpu.VMEM),
            ],
            out_specs=[
                pl.BlockSpec((features, wide), lambda i, place: (0, i)),
                pl.BlockSpec((hidden, wide), lambda i, place: (0, i)),
            ],
        ),
        out_shape=[
            jax.ShapeDtypeStruct((features, owned), jnp.bfloat16),
            jax.ShapeDtypeStruct((hidden, owned), jnp.float32),
        ],
        compiler_params=pltpu.CompilerParams(vmem_limit_bytes=24 * MIB),
        cost_estimate=pl.CostEstimate(flops=2_000_000_000, bytes_accessed=6 * MIB, transcendentals=0),
        name="first_arrived",
    )(place, ids, moved, weights, bias)


def gelu_and_slope(pre):
    c, k = 0.7978845608028654, 0.044715
    square = pre * pre
    t = jnp.tanh(c * pre * (1.0 + k * square))
    half = 0.5 * (1.0 + t)
    slope = half + 0.5 * pre * (1.0 - t * t) * (c * (1.0 + 3.0 * k * square))
    return pre * half, slope


def finish_kernel(
    place_ref, pre_hbm, second_hbm, first_hbm, weights_hbm, upstream_hbm, hidden_hbm, keep_hbm, send_hbm,
    pre_ref, second_ref, first_ref, weight_ref, upstream_ref, slope, hidden_ref, keep_ref, send_ref, load, leave,
):
    owned = pre_ref.shape[1]
    wide = 2 * BLOCK
    core, limit = place_ref[0], place_ref[2]

    load_weight = pltpu.make_async_copy(weights_hbm.at[1 - core], weight_ref, load.at[0])
    load_second = pltpu.make_async_copy(second_hbm, second_ref, load.at[1])
    load_pre = pltpu.make_async_copy(pre_hbm, pre_ref, load.at[2])
    load_upstream = pltpu.make_async_copy(upstream_hbm, upstream_ref, load.at[3])
    load_first = pltpu.make_async_copy(first_hbm, first_ref, load.at[4])
    early = [load_weight, load_second, load_pre, load_upstream]
    for copy in early + [load_first]:
        copy.start()
    for copy in early:
        copy.wait()

    for j in range(0, owned, wide):
        columns = slice(j, j + wide)
        active, back = gelu_and_slope(dot(weight_ref[...], second_ref[:, columns]) + pre_ref[:, columns])
        positions = j + lax.broadcasted_iota(jnp.int32, (1, wide), 1)
        valid = jnp.where(positions < limit, 1.0, 0.0)
        hidden_ref[:, columns] = (active * valid).astype(jnp.bfloat16)
        slope[:, columns] = (upstream_ref[:, columns].astype(jnp.float32) * back * valid).astype(jnp.bfloat16)
    leave_hidden = pltpu.make_async_copy(hidden_ref, hidden_hbm, leave.at[0])
    leave_hidden.start()

    owners, share, _ = keep_ref.shape
    group = 4

    def grads(left_ref, out_ref):
        for i in range(0, owners, group):
            total = dot(left_ref[i * share : (i + group) * share, :], slope[...], NT)
            out_ref[i : i + group] = total.reshape(group, share, -1).astype(out_ref.dtype)

    grads(second_ref, send_ref)
    leave_send = pltpu.make_async_copy(send_ref, send_hbm, leave.at[1])
    leave_send.start()
    load_first.wait()
    grads(first_ref, keep_ref)
    leave_keep = pltpu.make_async_copy(keep_ref, keep_hbm, leave.at[2])
    leave_keep.start()
    leave_hidden.wait()
    leave_send.wait()
    leave_keep.wait()


def finish(place, pre, second, first, weights, upstream, owners):
    hidden, owned = pre.shape
    features = second.shape[0]
    part = (owners, features // owners, hidden)
    anywhere = pl.BlockSpec(memory_space=pl.ANY)
    outs = [
        jax.ShapeDtypeStruct((hidden, owned), jnp.bfloat16),
        jax.ShapeDtypeStruct(part, jnp.float32),
        jax.ShapeDtypeStruct(part, jnp.bfloat16),
    ]
    return pl.pallas_call(
        finish_kernel,
        in_specs=[pl.BlockSpec(memory_space=pltpu.SMEM)] + [anywhere] * 5,
        out_specs=[anywhere] * 3,
        out_shape=outs,
        scratch_shapes=[pltpu.VMEM(a.shape, a.dtype) for a in (pre, second, first, weights[0], upstream)]
        + [pltpu.VMEM((hidden, owned), jnp.bfloat16)]
        + [pltpu.VMEM(a.shape, a.dtype) for a in outs]
        + [pltpu.SemaphoreType.DMA((5,)), pltpu.SemaphoreType.DMA((3,))],
        compiler_params=pltpu.CompilerParams(vmem_limit_bytes=WHOLE),
        cost_estimate=pl.CostEstimate(flops=2_000_000_000, bytes_accessed=9 * MIB, transcendentals=262144),
        name="finish",
    )(place, pre, second, first, weights, upstream)


def on_device(
    node_table, node_ids, block_lists, block_counts, tiles, batch_sizes, w_self, w_neigh, bias, cotangent
):
    owners = lax.axis_size(FEAT)
    rank, core = lax.axis_index(FEAT), lax.axis_index("core")
    table = jnp.swapaxes(node_table[0], 0, 1)
    width = table.shape[0]
    ids = node_ids[0].reshape(-1, BLOCK)
    owned = cotangent.shape[1]

    lists = jnp.transpose(block_lists, (2, 0, 1))
    place = jnp.stack([core, rank * (owned // BLOCK), batch_sizes[0] - rank * owned])
    operands = (core.reshape(1), lists, block_counts, ids, table, tiles[0], owners)
    weights = jnp.stack([w_self.T, w_neigh.T])

    first = outgoing(first_kernel, *operands, "first_outgoing")
    moved = lax.all_to_all(first, FEAT, split_axis=0, concat_axis=0, tiled=True)
    second = outgoing(second_kernel, *operands, "second_outgoing")
    second = lax.all_to_all(second, FEAT, split_axis=0, concat_axis=0, tiled=True)
    first, pre = arrived(place, ids, moved.reshape(-1, owned), weights, bias[:, None])
    second = second.reshape(-1, owned)
    hidden, keep, send = finish(place, pre, second, first, weights, cotangent[0].T, owners)

    got = lax.ppermute(send, "core", [(0, 1), (1, 0)])
    parts = lax.all_to_all((keep + got).astype(jnp.bfloat16), FEAT, split_axis=0, concat_axis=0, tiled=True)
    total = jnp.sum(parts, axis=0, dtype=jnp.float32)
    others = [lax.ppermute(total, "x", [(i, i ^ k) for i in range(4)]) for k in (1, 2, 3)]
    total = (total + others[0]) + (others[1] + others[2])
    other = lax.ppermute(total, "core", [(0, 1), (1, 0)])
    first_core = core == 0
    return (
        hidden.T[None],
        jnp.where(first_core, total, other),
        jnp.where(first_core, other, total),
    )


def solution(mesh):
    axes = Mesh(mesh.devices.reshape(4, 4, 4, 2), ("z", "y", "x", "core"))
    in_specs = (
        P(GRP, None, FEAT),
        P(GRP, None),
        P(GRP, None, None),
        P(GRP, None),
        P(GRP, None, None, None, None),
        P(GRP),
        P(),
        P(),
        P(),
        P(GRP, FEAT, None),
    )
    out_specs = (P(GRP, FEAT, None), P(FEAT, None), P(FEAT, None))
    return jax.shard_map(on_device, mesh=axes, in_specs=in_specs, out_specs=out_specs, check_vma=False)
```

```python
import jax
import jax.numpy as jnp
from jax import lax
from jax.experimental import pallas as pl
from jax.experimental.pallas import tpu as pltpu
from jax.sharding import Mesh, PartitionSpec as P

BLOCK = 128
MIB = 1 << 20
WHOLE = 60 * MIB
FEAT = ("z", "y")
GRP = ("x", "core")
NT = (((1,), (1,)), ((), ()))
NN = (((1,), (0,)), ((), ()))


def dot(left, right, dims=NN):
    return lax.dot_general(left, right, dims, preferred_element_type=jnp.float32)


def selector(within):
    rows = lax.broadcasted_iota(jnp.int32, (BLOCK, BLOCK), 0)
    return jnp.where(rows == within, 1.0, 0.0).astype(jnp.bfloat16)


def read_blocks(ids_ref, vector, which, sem):
    lanes = lax.broadcasted_iota(jnp.int32, (vector.shape[0], BLOCK), 1)
    first = jnp.where(lanes == 0, 1.0, 0.0).astype(jnp.bfloat16)
    blocks = lax.shift_right_logical(ids_ref[...], 7).astype(jnp.float32).astype(jnp.bfloat16)
    vector[...] = dot(first, blocks, NT).astype(jnp.int32)
    copy = pltpu.make_async_copy(vector, which, sem)
    copy.start()
    copy.wait()


def block_of(table, w):
    return table[:, pl.ds(pl.multiple_of(w * BLOCK, BLOCK), BLOCK)]


def in_run_order(chosen, ids_row):
    within = jnp.broadcast_to(jnp.bitwise_and(ids_row, BLOCK - 1), (8, BLOCK))
    chosen = chosen.astype(jnp.float32)
    rows = [jnp.take_along_axis(chosen[i : i + 8], within, axis=1) for i in range(0, chosen.shape[0], 8)]
    return jnp.concatenate(rows, axis=0).astype(jnp.bfloat16)


def outgoing_kernel(
    lists_ref, counts_ref, ids_ref, table_hbm, tiles_hbm, out_hbm, rows, table, tiles, vector, which, load, leave
):
    blocks = ids_ref.shape[0]
    owners, width, owned = rows.shape
    width = width // 2
    per = owned // BLOCK
    slots, dst_blocks = lists_ref.shape[0], lists_ref.shape[2]
    together = 4

    def load_tiles(r):
        part = pl.ds(r * per, per)
        return pltpu.make_async_copy(tiles_hbm.at[part], tiles.at[part], load.at[r])

    known = table.at[:, pl.ds(0, table_hbm.shape[1])]
    load_table = pltpu.make_async_copy(table_hbm, known, load.at[owners + 1])
    load_table.start()
    for r in range(owners):
        load_tiles(r).start()
    table[:, table_hbm.shape[1] :] = jnp.zeros((width, BLOCK), table.dtype)
    read_blocks(ids_ref, vector, which, load.at[owners])
    load_table.wait()

    def aggregated(d):
        count = counts_ref[0, d]
        left = []
        for s in range(slots):
            used = s < count
            n = lists_ref[s, 0, d]
            w = jnp.where(used, which[0, n], blocks)
            source = in_run_order(block_of(table, w), ids_ref[pl.ds(n, 1), :])
            ones = jnp.full((16, BLOCK), jnp.where(used, 1.0, 0.0), jnp.float32).astype(jnp.bfloat16)
            left.append(jnp.concatenate([source, ones], axis=0))
        right = jnp.concatenate([tiles[d, s] for s in range(slots)], axis=1)
        total = dot(jnp.concatenate(left, axis=1), right, NT)
        return (total[:width] * (1.0 / total[width : width + 1])).astype(jnp.bfloat16)

    def some(i, carry):
        for k in range(together):
            load_tiles(i * together + k).wait()
        first = i * together * per
        results = [aggregated(first + k) for k in range(together * per)]
        own = [block_of(table, which[0, first + k]) for k in range(together * per)]
        for k in range(together * per):
            r, columns = i * together + k // per, slice((k % per) * BLOCK, (k % per + 1) * BLOCK)
            rows[r, :width, columns] = own[k]
            rows[r, width:, columns] = results[k]
        for k in range(together):
            r = i * together + k
            pltpu.make_async_copy(rows.at[r], out_hbm.at[r], leave.at[r]).start()
        return carry

    lax.fori_loop(0, dst_blocks // per // together, some, 0)
    for r in range(owners):
        pltpu.make_async_copy(rows.at[r], out_hbm.at[r], leave.at[r]).wait()


def outgoing(lists, counts, ids, table, tiles, owners):
    width, rows = table.shape
    blocks = rows // BLOCK
    smem, vmem = pl.BlockSpec(memory_space=pltpu.SMEM), pl.BlockSpec(memory_space=pltpu.VMEM)
    anywhere = pl.BlockSpec(memory_space=pl.ANY)
    out = (owners, 2 * width, tiles.shape[0] // owners * BLOCK)
    return pl.pallas_call(
        outgoing_kernel,
        in_specs=[smem, smem, vmem, anywhere, anywhere],
        out_specs=anywhere,
        out_shape=jax.ShapeDtypeStruct(out, jnp.bfloat16),
        scratch_shapes=[
            pltpu.VMEM(out, jnp.bfloat16),
            pltpu.VMEM((width, rows + BLOCK), jnp.bfloat16),
            pltpu.VMEM(tiles.shape, jnp.bfloat16),
            pltpu.VMEM((8, blocks), jnp.int32),
            pltpu.SMEM((8, blocks), jnp.int32),
            pltpu.SemaphoreType.DMA((owners + 2,)),
            pltpu.SemaphoreType.DMA((owners,)),
        ],
        compiler_params=pltpu.CompilerParams(vmem_limit_bytes=WHOLE),
        cost_estimate=pl.CostEstimate(flops=4_000_000_000, bytes_accessed=20 * MIB, transcendentals=0),
        name="pick_and_aggregate",
    )(lists, counts, ids, table, tiles)


def gelu_and_slope(pre):
    c, k = 0.7978845608028654, 0.044715
    square = pre * pre
    t = jnp.tanh(c * pre * (1.0 + k * square))
    half = 0.5 * (1.0 + t)
    slope = half + 0.5 * pre * (1.0 - t * t) * (c * (1.0 + 3.0 * k * square))
    return pre * half, slope


def move_lanes(rows, order):
    order = jnp.broadcast_to(order, (8, BLOCK))
    moved = [jnp.take_along_axis(rows[i : i + 8], order, axis=1) for i in range(0, rows.shape[0], 8)]
    return jnp.concatenate(moved, axis=0)


def finish_kernel(
    place_ref, bias_ref, ids_hbm, moved_hbm, weights_hbm, upstream_hbm, hidden_hbm, keep_hbm, send_hbm,
    ids_ref, rows, weights, upstream_ref, slopes, hidden_ref, keep_ref, send_ref, load, leave,
):
    owners, share, owned = rows.shape[1:]
    features = owners * share
    per = owned // BLOCK
    core, rank, limit = place_ref[0], place_ref[1], place_ref[2]
    own_slot, agg_slot = core, 1 - core

    load_ids = pltpu.make_async_copy(ids_hbm.at[pl.ds(pl.multiple_of(rank * per, per), per)], ids_ref, load.at[0])
    load_weights = pltpu.make_async_copy(weights_hbm, weights, load.at[1])
    half = owned // 2
    load_rows = []
    for h in range(2):
        columns = slice(h * half, (h + 1) * half)
        for k, slot in enumerate((own_slot, agg_slot)):
            load_rows.append(
                pltpu.make_async_copy(
                    moved_hbm.at[:, k * share : (k + 1) * share, columns],
                    rows.at[slot, :, :, columns],
                    load.at[2 + 2 * h + k],
                )
            )
    load_upstream = pltpu.make_async_copy(upstream_hbm, upstream_ref, load.at[6])
    load_ids.start()
    load_weights.start()
    load_rows[0].start()
    load_rows[1].start()
    load_upstream.start()
    load_rows[2].start()
    load_rows[3].start()

    load_ids.wait()
    lanes = lax.broadcasted_iota(jnp.int32, (8, BLOCK), 1).astype(jnp.bfloat16)
    orders = [jnp.bitwise_and(ids_ref[b : b + 1, :], BLOCK - 1) for b in range(per)]
    inverse = [dot(lanes, selector(order), NT).astype(jnp.int32) for order in orders]
    load_weights.wait()
    load_upstream.wait()

    def rows_of(slot, columns):
        return rows[slot, :, :, columns].reshape(features, BLOCK)

    for h in range(2):
        load_rows[2 * h].wait()
        load_rows[2 * h + 1].wait()
        for b in range(h * per // 2, (h + 1) * per // 2):
            columns = slice(b * BLOCK, (b + 1) * BLOCK)
            own = move_lanes(dot(weights[0], rows_of(own_slot, columns)), orders[b])
            pre = own + dot(weights[1], rows_of(agg_slot, columns)) + bias_ref[...]
            active, back = gelu_and_slope(pre)
            positions = b * BLOCK + lax.broadcasted_iota(jnp.int32, (1, BLOCK), 1)
            valid = jnp.where(positions < limit, 1.0, 0.0)
            hidden_ref[:, columns] = (active * valid).astype(jnp.bfloat16)
            slope = (upstream_ref[:, columns].astype(jnp.float32) * back * valid).astype(jnp.bfloat16)
            slopes[agg_slot, :, columns] = slope
            slopes[own_slot, :, columns] = move_lanes(slope.astype(jnp.float32), inverse[b]).astype(jnp.bfloat16)
    leave_hidden = pltpu.make_async_copy(hidden_ref, hidden_hbm, leave.at[0])
    leave_hidden.start()

    group = 4

    def grads(slot, out_ref):
        for i in range(0, owners, group):
            left = rows[slot, i : i + group].reshape(group * share, owned)
            total = dot(left, slopes[slot], NT)
            out_ref[i : i + group] = total.reshape(group, share, -1).astype(out_ref.dtype)

    grads(1, send_ref)
    leave_send = pltpu.make_async_copy(send_ref, send_hbm, leave.at[1])
    leave_send.start()
    grads(0, keep_ref)
    leave_keep = pltpu.make_async_copy(keep_ref, keep_hbm, leave.at[2])
    leave_keep.start()
    leave_hidden.wait()
    leave_send.wait()
    leave_keep.wait()


def finish(place, bias, ids, moved, weights, upstream):
    owners, share, owned = moved.shape[0], moved.shape[1] // 2, moved.shape[2]
    hidden = weights.shape[1]
    part = (owners, share, hidden)
    anywhere = pl.BlockSpec(memory_space=pl.ANY)
    outs = [
        jax.ShapeDtypeStruct((hidden, owned), jnp.bfloat16),
        jax.ShapeDtypeStruct(part, jnp.float32),
        jax.ShapeDtypeStruct(part, jnp.bfloat16),
    ]
    return pl.pallas_call(
        finish_kernel,
        in_specs=[pl.BlockSpec(memory_space=pltpu.SMEM), pl.BlockSpec(memory_space=pltpu.VMEM)] + [anywhere] * 4,
        out_specs=[anywhere] * 3,
        out_shape=outs,
        scratch_shapes=[
            pltpu.VMEM((owned // BLOCK, BLOCK), jnp.int32),
            pltpu.VMEM((2, owners, share, owned), jnp.bfloat16),
            pltpu.VMEM(weights.shape, jnp.bfloat16),
            pltpu.VMEM(upstream.shape, jnp.bfloat16),
            pltpu.VMEM((2, hidden, owned), jnp.bfloat16),
        ]
        + [pltpu.VMEM(a.shape, a.dtype) for a in outs]
        + [pltpu.SemaphoreType.DMA((7,)), pltpu.SemaphoreType.DMA((3,))],
        compiler_params=pltpu.CompilerParams(vmem_limit_bytes=WHOLE),
        cost_estimate=pl.CostEstimate(flops=2_000_000_000, bytes_accessed=9 * MIB, transcendentals=262144),
        name="finish",
    )(place, bias, ids, moved, weights, upstream)


def on_device(
    node_table, node_ids, block_lists, block_counts, tiles, batch_sizes, w_self, w_neigh, bias, cotangent
):
    owners = lax.axis_size(FEAT)
    rank, core = lax.axis_index(FEAT), lax.axis_index("core")
    table = jnp.swapaxes(node_table[0], 0, 1)
    width = table.shape[0]
    ids = node_ids[0].reshape(-1, BLOCK)
    owned = cotangent.shape[1]

    lists = jnp.transpose(block_lists, (2, 0, 1))
    place = jnp.stack([core, rank, batch_sizes[0] - rank * owned])
    weights = jnp.stack([w_self.T, w_neigh.T])

    rows = outgoing(lists, block_counts, ids, table, tiles[0], owners)
    moved = lax.all_to_all(rows, FEAT, split_axis=0, concat_axis=0, tiled=True)
    hidden, keep, send = finish(place, bias[:, None], ids, moved, weights, cotangent[0].T)

    got = lax.ppermute(send, "core", [(0, 1), (1, 0)])
    parts = lax.all_to_all((keep + got).astype(jnp.bfloat16), FEAT, split_axis=0, concat_axis=0, tiled=True)
    total = jnp.sum(parts, axis=0, dtype=jnp.float32)
    others = [lax.ppermute(total, "x", [(i, i ^ k) for i in range(4)]) for k in (1, 2, 3)]
    total = (total + others[0]) + (others[1] + others[2])
    other = lax.ppermute(total, "core", [(0, 1), (1, 0)])
    first_core = core == 0
    return (
        hidden.T[None],
        jnp.where(first_core, total, other),
        jnp.where(first_core, other, total),
    )


def solution(mesh):
    axes = Mesh(mesh.devices.reshape(4, 4, 4, 2), ("z", "y", "x", "core"))
    in_specs = (
        P(GRP, None, FEAT),
        P(GRP, None),
        P(GRP, None, None),
        P(GRP, None),
        P(GRP, None, None, None, None),
        P(GRP),
        P(),
        P(),
        P(),
        P(GRP, FEAT, None),
    )
    out_specs = (P(GRP, FEAT, None), P(FEAT, None), P(FEAT, None))
    return jax.shard_map(on_device, mesh=axes, in_specs=in_specs, out_specs=out_specs, check_vma=False)
```

```python
import jax
import jax.numpy as jnp
from jax import lax
from jax.experimental import pallas as pl
from jax.experimental.pallas import tpu as pltpu
from jax.sharding import Mesh, PartitionSpec as P

BLOCK = 128
MIB = 1 << 20
WHOLE = 60 * MIB
FEAT = ("z", "y")
GRP = ("x", "core")
NT = (((1,), (1,)), ((), ()))
NN = (((1,), (0,)), ((), ()))


def dot(left, right, dims=NN):
    return lax.dot_general(left, right, dims, preferred_element_type=jnp.float32)


def selector(within):
    rows = lax.broadcasted_iota(jnp.int32, (BLOCK, BLOCK), 0)
    return jnp.where(rows == within, 1.0, 0.0).astype(jnp.bfloat16)


def read_blocks(ids_ref, vector, which, sem):
    lanes = lax.broadcasted_iota(jnp.int32, (vector.shape[0], BLOCK), 1)
    first = jnp.where(lanes == 0, 1.0, 0.0).astype(jnp.bfloat16)
    blocks = lax.shift_right_logical(ids_ref[...], 7).astype(jnp.float32).astype(jnp.bfloat16)
    vector[...] = dot(first, blocks, NT).astype(jnp.int32)
    copy = pltpu.make_async_copy(vector, which, sem)
    copy.start()
    copy.wait()


def block_of(table, w):
    return table[:, pl.ds(pl.multiple_of(w * BLOCK, BLOCK), BLOCK)]


def in_run_order(chosen, ids_row):
    within = jnp.broadcast_to(jnp.bitwise_and(ids_row, BLOCK - 1), (8, BLOCK))
    chosen = chosen.astype(jnp.float32)
    rows = [jnp.take_along_axis(chosen[i : i + 8], within, axis=1) for i in range(0, chosen.shape[0], 8)]
    return jnp.concatenate(rows, axis=0).astype(jnp.bfloat16)


def pick_kernel(ids_ref, table_hbm, out_ref, vector, which, load):
    owners, _, owned = out_ref.shape
    per = owned // BLOCK
    read_blocks(ids_ref, vector, which, load.at[1])

    def start(r, carry):
        for b in range(per):
            pltpu.make_async_copy(
                block_of(table_hbm.at, which[0, r * per + b]),
                out_ref.at[r, :, b * BLOCK : (b + 1) * BLOCK],
                load.at[0],
            ).start()
        return carry

    lax.fori_loop(0, owners, start, 0)
    pltpu.make_async_copy(out_ref, out_ref, load.at[0]).wait()


def pick(ids, table, owners):
    width, rows = table.shape
    blocks = rows // BLOCK
    vmem, anywhere = pl.BlockSpec(memory_space=pltpu.VMEM), pl.BlockSpec(memory_space=pl.ANY)
    return pl.pallas_call(
        pick_kernel,
        in_specs=[vmem, anywhere],
        out_specs=vmem,
        out_shape=jax.ShapeDtypeStruct((owners, width, rows // 2 // owners), jnp.bfloat16),
        scratch_shapes=[
            pltpu.VMEM((8, blocks), jnp.int32),
            pltpu.SMEM((8, blocks), jnp.int32),
            pltpu.SemaphoreType.DMA((2,)),
        ],
        compiler_params=pltpu.CompilerParams(vmem_limit_bytes=WHOLE),
        cost_estimate=pl.CostEstimate(flops=0, bytes_accessed=4 * MIB, transcendentals=0),
        name="pick",
    )(ids, table)


def aggregate_kernel(
    lists_ref, counts_ref, ids_ref, table_hbm, tiles_hbm, out_hbm, rows, table, tiles, vector, which, load, leave
):
    blocks = ids_ref.shape[0]
    owners, width, _ = rows.shape
    dst_blocks, slots = tiles.shape[0], tiles.shape[1]
    per = dst_blocks // owners
    together = 4

    def load_tiles(r):
        part = pl.ds(r * per, per)
        return pltpu.make_async_copy(tiles_hbm.at[part], tiles.at[part], load.at[r])

    known = table.at[:, pl.ds(0, table_hbm.shape[1])]
    load_table = pltpu.make_async_copy(table_hbm, known, load.at[owners + 1])
    load_table.start()
    for r in range(owners):
        load_tiles(r).start()
    table[:, table_hbm.shape[1] :] = jnp.zeros((width, BLOCK), table.dtype)
    read_blocks(ids_ref, vector, which, load.at[owners])
    load_table.wait()

    def one(d):
        count = counts_ref[0, d]
        left = []
        for s in range(slots):
            used = s < count
            n = lists_ref[s, 0, d]
            w = jnp.where(used, which[0, n], blocks)
            source = in_run_order(block_of(table, w), ids_ref[pl.ds(n, 1), :])
            ones = jnp.full((16, BLOCK), jnp.where(used, 1.0, 0.0), jnp.float32).astype(jnp.bfloat16)
            left.append(jnp.concatenate([source, ones], axis=0))
        right = jnp.concatenate([tiles[d, s] for s in range(slots)], axis=1)
        total = dot(jnp.concatenate(left, axis=1), right, NT)
        return (total[:width] * (1.0 / total[width : width + 1])).astype(jnp.bfloat16)

    def some(i, carry):
        for k in range(together):
            load_tiles(i * together + k).wait()
        results = [one(i * together * per + k) for k in range(together * per)]
        for k in range(together * per):
            rows[i * together + k // per, :, (k % per) * BLOCK : (k % per + 1) * BLOCK] = results[k]
        for k in range(together):
            r = i * together + k
            pltpu.make_async_copy(rows.at[r], out_hbm.at[r], leave.at[r]).start()
        return carry

    lax.fori_loop(0, owners // together, some, 0)
    for r in range(owners):
        pltpu.make_async_copy(rows.at[r], out_hbm.at[r], leave.at[r]).wait()


def aggregate(lists, counts, ids, table, tiles, owners):
    width, rows = table.shape
    blocks = rows // BLOCK
    smem, vmem = pl.BlockSpec(memory_space=pltpu.SMEM), pl.BlockSpec(memory_space=pltpu.VMEM)
    anywhere = pl.BlockSpec(memory_space=pl.ANY)
    out = (owners, width, tiles.shape[0] // owners * BLOCK)
    return pl.pallas_call(
        aggregate_kernel,
        in_specs=[smem, smem, vmem, anywhere, anywhere],
        out_specs=anywhere,
        out_shape=jax.ShapeDtypeStruct(out, jnp.bfloat16),
        scratch_shapes=[
            pltpu.VMEM(out, jnp.bfloat16),
            pltpu.VMEM((width, rows + BLOCK), jnp.bfloat16),
            pltpu.VMEM(tiles.shape, jnp.bfloat16),
            pltpu.VMEM((8, blocks), jnp.int32),
            pltpu.SMEM((8, blocks), jnp.int32),
            pltpu.SemaphoreType.DMA((owners + 2,)),
            pltpu.SemaphoreType.DMA((owners,)),
        ],
        compiler_params=pltpu.CompilerParams(vmem_limit_bytes=WHOLE),
        cost_estimate=pl.CostEstimate(flops=4_000_000_000, bytes_accessed=20 * MIB, transcendentals=0),
        name="aggregate",
    )(lists, counts, ids, table, tiles)


def arrived_kernel(place_ref, ids_ref, moved_ref, weight_ref, bias_ref, rows_ref, pre_ref):
    step = pl.program_id(0)
    per = rows_ref.shape[1] // BLOCK
    for b in range(per):
        row = place_ref[1] + step * per + b
        within = jnp.bitwise_and(ids_ref[pl.ds(row, 1), :], BLOCK - 1)
        columns = slice(b * BLOCK, (b + 1) * BLOCK)
        rows_ref[:, columns] = dot(moved_ref[:, columns], selector(within)).astype(jnp.bfloat16)
    pre_ref[...] = dot(weight_ref[...], rows_ref[...]) + bias_ref[...]


def arrived(place, ids, moved, weight, bias):
    features, owned = moved.shape
    hidden = weight.shape[0]
    wide = 2 * BLOCK
    return pl.pallas_call(
        arrived_kernel,
        grid_spec=pltpu.PrefetchScalarGridSpec(
            num_scalar_prefetch=1,
            grid=(owned // wide,),
            in_specs=[
                pl.BlockSpec(memory_space=pltpu.VMEM),
                pl.BlockSpec((features, wide), lambda i, place: (0, i)),
                pl.BlockSpec(memory_space=pltpu.VMEM),
                pl.BlockSpec(memory_space=pltpu.VMEM),
            ],
            out_specs=[
                pl.BlockSpec((features, wide), lambda i, place: (0, i)),
                pl.BlockSpec((hidden, wide), lambda i, place: (0, i)),
            ],
        ),
        out_shape=[
            jax.ShapeDtypeStruct((features, owned), jnp.bfloat16),
            jax.ShapeDtypeStruct((hidden, owned), jnp.float32),
        ],
        compiler_params=pltpu.CompilerParams(vmem_limit_bytes=24 * MIB),
        cost_estimate=pl.CostEstimate(flops=2_000_000_000, bytes_accessed=6 * MIB, transcendentals=0),
        name="own_arrived",
    )(place, ids, moved, weight, bias)


def gelu_and_slope(pre):
    c, k = 0.7978845608028654, 0.044715
    square = pre * pre
    t = jnp.tanh(c * pre * (1.0 + k * square))
    half = 0.5 * (1.0 + t)
    slope = half + 0.5 * pre * (1.0 - t * t) * (c * (1.0 + 3.0 * k * square))
    return pre * half, slope


def finish_kernel(
    place_ref, pre_hbm, agg_hbm, own_hbm, weight_hbm, upstream_hbm, hidden_hbm, keep_hbm, send_hbm,
    pre_ref, rows, weight_ref, upstream_ref, slope, hidden_ref, keep_ref, send_ref, load, leave,
):
    owned = pre_ref.shape[1]
    wide = 2 * BLOCK
    core, limit = place_ref[0], place_ref[2]

    own_slot, agg_slot = core, 1 - core

    load_weight = pltpu.make_async_copy(weight_hbm, weight_ref, load.at[0])
    load_agg = pltpu.make_async_copy(agg_hbm, rows.at[agg_slot], load.at[1])
    load_pre = pltpu.make_async_copy(pre_hbm, pre_ref, load.at[2])
    load_upstream = pltpu.make_async_copy(upstream_hbm, upstream_ref, load.at[3])
    load_own = pltpu.make_async_copy(own_hbm, rows.at[own_slot], load.at[4])
    early = [load_weight, load_agg, load_pre, load_upstream]
    for copy in early + [load_own]:
        copy.start()
    for copy in early:
        copy.wait()

    for j in range(0, owned, wide):
        columns = slice(j, j + wide)
        active, back = gelu_and_slope(dot(weight_ref[...], rows[agg_slot, :, columns]) + pre_ref[:, columns])
        positions = j + lax.broadcasted_iota(jnp.int32, (1, wide), 1)
        valid = jnp.where(positions < limit, 1.0, 0.0)
        hidden_ref[:, columns] = (active * valid).astype(jnp.bfloat16)
        slope[:, columns] = (upstream_ref[:, columns].astype(jnp.float32) * back * valid).astype(jnp.bfloat16)
    leave_hidden = pltpu.make_async_copy(hidden_ref, hidden_hbm, leave.at[0])
    leave_hidden.start()

    owners, share, _ = keep_ref.shape
    group = 4

    def grads(slot, out_ref):
        for i in range(0, owners, group):
            total = dot(rows[slot, i * share : (i + group) * share, :], slope[...], NT)
            out_ref[i : i + group] = total.reshape(group, share, -1).astype(out_ref.dtype)

    load_own.wait()
    grads(1, send_ref)
    leave_send = pltpu.make_async_copy(send_ref, send_hbm, leave.at[1])
    leave_send.start()
    grads(0, keep_ref)
    leave_keep = pltpu.make_async_copy(keep_ref, keep_hbm, leave.at[2])
    leave_keep.start()
    leave_hidden.wait()
    leave_send.wait()
    leave_keep.wait()


def finish(place, pre, agg, own, weight, upstream, owners):
    hidden, owned = pre.shape
    features = agg.shape[0]
    part = (owners, features // owners, hidden)
    anywhere = pl.BlockSpec(memory_space=pl.ANY)
    outs = [
        jax.ShapeDtypeStruct((hidden, owned), jnp.bfloat16),
        jax.ShapeDtypeStruct(part, jnp.float32),
        jax.ShapeDtypeStruct(part, jnp.bfloat16),
    ]
    return pl.pallas_call(
        finish_kernel,
        in_specs=[pl.BlockSpec(memory_space=pltpu.SMEM)] + [anywhere] * 5,
        out_specs=[anywhere] * 3,
        out_shape=outs,
        scratch_shapes=[
            pltpu.VMEM(pre.shape, pre.dtype),
            pltpu.VMEM((2, features, owned), jnp.bfloat16),
            pltpu.VMEM(weight.shape, weight.dtype),
            pltpu.VMEM(upstream.shape, upstream.dtype),
            pltpu.VMEM((hidden, owned), jnp.bfloat16),
        ]
        + [pltpu.VMEM(a.shape, a.dtype) for a in outs]
        + [pltpu.SemaphoreType.DMA((5,)), pltpu.SemaphoreType.DMA((3,))],
        compiler_params=pltpu.CompilerParams(vmem_limit_bytes=WHOLE),
        cost_estimate=pl.CostEstimate(flops=2_000_000_000, bytes_accessed=9 * MIB, transcendentals=262144),
        name="finish",
    )(place, pre, agg, own, weight, upstream)


def on_device(
    node_table, node_ids, block_lists, block_counts, tiles, batch_sizes, w_self, w_neigh, bias, cotangent
):
    owners = lax.axis_size(FEAT)
    rank, core = lax.axis_index(FEAT), lax.axis_index("core")
    table = jnp.swapaxes(node_table[0], 0, 1)
    width = table.shape[0]
    ids = node_ids[0].reshape(-1, BLOCK)
    owned = cotangent.shape[1]

    lists = jnp.transpose(block_lists, (2, 0, 1))
    place = jnp.stack([core, rank * (owned // BLOCK), batch_sizes[0] - rank * owned])

    mine = pick(ids, table, owners)
    moved = lax.all_to_all(mine, FEAT, split_axis=0, concat_axis=0, tiled=True)
    agg = aggregate(lists, block_counts, ids, table, tiles[0], owners)
    agg = lax.all_to_all(agg, FEAT, split_axis=0, concat_axis=0, tiled=True).reshape(-1, owned)
    own, pre = arrived(place, ids, moved.reshape(-1, owned), w_self.T, bias[:, None])
    hidden, keep, send = finish(place, pre, agg, own, w_neigh.T, cotangent[0].T, owners)

    got = lax.ppermute(send, "core", [(0, 1), (1, 0)])
    parts = lax.all_to_all((keep + got).astype(jnp.bfloat16), FEAT, split_axis=0, concat_axis=0, tiled=True)
    total = jnp.sum(parts, axis=0, dtype=jnp.float32).astype(jnp.bfloat16)
    others = [lax.ppermute(total, "x", [(i, i ^ k) for i in range(4)]) for k in (1, 2, 3)]
    total, *others = [term.astype(jnp.float32) for term in (total, *others)]
    total = (total + others[0]) + (others[1] + others[2])
    other = lax.ppermute(total, "core", [(0, 1), (1, 0)])
    first_core = core == 0
    return (
        hidden.T[None],
        jnp.where(first_core, total, other),
        jnp.where(first_core, other, total),
    )


def solution(mesh):
    axes = Mesh(mesh.devices.reshape(4, 4, 4, 2), ("z", "y", "x", "core"))
    in_specs = (
        P(GRP, None, FEAT),
        P(GRP, None),
        P(GRP, None, None),
        P(GRP, None),
        P(GRP, None, None, None, None),
        P(GRP),
        P(),
        P(),
        P(),
        P(GRP, FEAT, None),
    )
    out_specs = (P(GRP, FEAT, None), P(FEAT, None), P(FEAT, None))
    return jax.shard_map(on_device, mesh=axes, in_specs=in_specs, out_specs=out_specs, check_vma=False)
```

```python
import jax
import jax.numpy as jnp
from jax import lax
from jax.experimental import pallas as pl
from jax.experimental.pallas import tpu as pltpu
from jax.sharding import Mesh, PartitionSpec as P

BLOCK = 128
MIB = 1 << 20
WHOLE = 60 * MIB
FEAT = ("z", "y")
GRP = ("x", "core")
NT = (((1,), (1,)), ((), ()))
NN = (((1,), (0,)), ((), ()))


def dot(left, right, dims=NN):
    return lax.dot_general(left, right, dims, preferred_element_type=jnp.float32)


def selector(within):
    rows = lax.broadcasted_iota(jnp.int32, (BLOCK, BLOCK), 0)
    return jnp.where(rows == within, 1.0, 0.0).astype(jnp.bfloat16)


def read_blocks(ids_ref, vector, which, sem):
    lanes = lax.broadcasted_iota(jnp.int32, (vector.shape[0], BLOCK), 1)
    first = jnp.where(lanes == 0, 1.0, 0.0).astype(jnp.bfloat16)
    blocks = lax.shift_right_logical(ids_ref[...], 7).astype(jnp.float32).astype(jnp.bfloat16)
    vector[...] = dot(first, blocks, NT).astype(jnp.int32)
    copy = pltpu.make_async_copy(vector, which, sem)
    copy.start()
    copy.wait()


def block_of(table, w):
    return table[:, pl.ds(pl.multiple_of(w * BLOCK, BLOCK), BLOCK)]


def in_run_order(chosen, ids_row):
    within = jnp.broadcast_to(jnp.bitwise_and(ids_row, BLOCK - 1), (8, BLOCK))
    chosen = chosen.astype(jnp.float32)
    rows = [jnp.take_along_axis(chosen[i : i + 8], within, axis=1) for i in range(0, chosen.shape[0], 8)]
    return jnp.concatenate(rows, axis=0).astype(jnp.bfloat16)


def pick_blocks(ids_ref, table_hbm, out_hbm, rows, vector, which, load, leave):
    owners, _, owned = rows.shape
    per = owned // BLOCK
    read_blocks(ids_ref, vector, which, load.at[owners])

    def start(r, carry):
        for b in range(per):
            pltpu.make_async_copy(
                block_of(table_hbm.at, which[0, r * per + b]),
                rows.at[r, :, b * BLOCK : (b + 1) * BLOCK],
                load.at[r],
            ).start()
        return carry

    lax.fori_loop(0, owners, start, 0)
    for r in range(owners):
        pltpu.make_async_copy(rows.at[r], rows.at[r], load.at[r]).wait()
        pltpu.make_async_copy(rows.at[r], out_hbm.at[r], leave.at[r]).start()
    for r in range(owners):
        pltpu.make_async_copy(rows.at[r], out_hbm.at[r], leave.at[r]).wait()


def place_blocks(ids_ref, table_hbm, out_hbm, rows, table, vector, which, load, leave):
    owners, _, owned = rows.shape
    per = owned // BLOCK
    known = table.at[:, pl.ds(0, table_hbm.shape[1])]
    load_table = pltpu.make_async_copy(table_hbm, known, load.at[0])
    load_table.start()
    read_blocks(ids_ref, vector, which, load.at[owners])
    load_table.wait()

    def owner(r, carry):
        placed = []
        for b in range(per):
            n = r * per + b
            placed.append(in_run_order(block_of(table, which[0, n]), ids_ref[pl.ds(n, 1), :]))
        for b in range(per):
            rows[r, :, b * BLOCK : (b + 1) * BLOCK] = placed[b]
        pltpu.make_async_copy(rows.at[r], out_hbm.at[r], leave.at[r]).start()
        return carry

    lax.fori_loop(0, owners, owner, 0)
    for r in range(owners):
        pltpu.make_async_copy(rows.at[r], out_hbm.at[r], leave.at[r]).wait()


def aggregate_blocks(
    lists_ref, counts_ref, ids_ref, table_hbm, tiles_hbm, out_hbm, rows, table, tiles, vector, which, load, leave
):
    blocks = ids_ref.shape[0]
    owners, width, _ = rows.shape
    dst_blocks, slots = tiles.shape[0], tiles.shape[1]
    per = dst_blocks // owners
    together = 4

    def load_tiles(r):
        part = pl.ds(r * per, per)
        return pltpu.make_async_copy(tiles_hbm.at[part], tiles.at[part], load.at[r])

    known = table.at[:, pl.ds(0, table_hbm.shape[1])]
    load_table = pltpu.make_async_copy(table_hbm, known, load.at[owners + 1])
    load_table.start()
    for r in range(together):
        load_tiles(r).start()
    table[:, table_hbm.shape[1] :] = jnp.zeros((width, BLOCK), table.dtype)
    read_blocks(ids_ref, vector, which, load.at[owners])
    load_table.wait()
    for r in range(together, owners):
        load_tiles(r).start()

    def one(d):
        count = counts_ref[0, d]
        left = []
        for s in range(slots):
            used = s < count
            n = lists_ref[s, 0, d]
            w = jnp.where(used, which[0, n], blocks)
            source = in_run_order(block_of(table, w), ids_ref[pl.ds(n, 1), :])
            ones = jnp.full((16, BLOCK), jnp.where(used, 1.0, 0.0), jnp.float32).astype(jnp.bfloat16)
            left.append(jnp.concatenate([source, ones], axis=0))
        right = jnp.concatenate([tiles[d, s] for s in range(slots)], axis=1)
        total = dot(jnp.concatenate(left, axis=1), right, NT)
        return (total[:width] * (1.0 / total[width : width + 1])).astype(jnp.bfloat16)

    def some(i, carry):
        for k in range(together):
            load_tiles(i * together + k).wait()
        results = [one(i * together * per + k) for k in range(together * per)]
        for k in range(together * per):
            rows[i * together + k // per, :, (k % per) * BLOCK : (k % per + 1) * BLOCK] = results[k]
        for k in range(together):
            r = i * together + k
            pltpu.make_async_copy(rows.at[r], out_hbm.at[r], leave.at[r]).start()
        return carry

    lax.fori_loop(0, owners // together, some, 0)
    for r in range(owners):
        pltpu.make_async_copy(rows.at[r], out_hbm.at[r], leave.at[r]).wait()


def first_kernel(
    core_ref, lists_ref, counts_ref, ids_ref, table_hbm, tiles_hbm, out_hbm,
    rows, table, tiles, vector, which, load, leave,
):
    @pl.when(core_ref[0] == 0)
    def _():
        pick_blocks(ids_ref, table_hbm, out_hbm, rows, vector, which, load, leave)

    @pl.when(core_ref[0] == 1)
    def _():
        aggregate_blocks(
            lists_ref, counts_ref, ids_ref, table_hbm, tiles_hbm, out_hbm,
            rows, table, tiles, vector, which, load, leave,
        )


def second_kernel(
    core_ref, lists_ref, counts_ref, ids_ref, table_hbm, tiles_hbm, out_hbm,
    rows, table, tiles, vector, which, load, leave,
):
    @pl.when(core_ref[0] == 1)
    def _():
        place_blocks(ids_ref, table_hbm, out_hbm, rows, table, vector, which, load, leave)

    @pl.when(core_ref[0] == 0)
    def _():
        aggregate_blocks(
            lists_ref, counts_ref, ids_ref, table_hbm, tiles_hbm, out_hbm,
            rows, table, tiles, vector, which, load, leave,
        )


def outgoing(kernel, core, lists, counts, ids, table, tiles, owners, name):
    width, rows = table.shape
    blocks = rows // BLOCK
    smem, vmem = pl.BlockSpec(memory_space=pltpu.SMEM), pl.BlockSpec(memory_space=pltpu.VMEM)
    anywhere = pl.BlockSpec(memory_space=pl.ANY)
    out = (owners, width, tiles.shape[0] // owners * BLOCK)
    return pl.pallas_call(
        kernel,
        in_specs=[smem, smem, smem, vmem, anywhere, anywhere],
        out_specs=anywhere,
        out_shape=jax.ShapeDtypeStruct(out, jnp.bfloat16),
        scratch_shapes=[
            pltpu.VMEM(out, jnp.bfloat16),
            pltpu.VMEM((width, rows + BLOCK), jnp.bfloat16),
            pltpu.VMEM(tiles.shape, jnp.bfloat16),
            pltpu.VMEM((8, blocks), jnp.int32),
            pltpu.SMEM((8, blocks), jnp.int32),
            pltpu.SemaphoreType.DMA((owners + 2,)),
            pltpu.SemaphoreType.DMA((owners,)),
        ],
        compiler_params=pltpu.CompilerParams(vmem_limit_bytes=WHOLE),
        cost_estimate=pl.CostEstimate(flops=4_000_000_000, bytes_accessed=20 * MIB, transcendentals=0),
        name=name,
    )(core, lists, counts, ids, table, tiles)


def arrived_kernel(place_ref, ids_ref, moved_ref, weight_ref, bias_ref, rows_ref, pre_ref):
    step = pl.program_id(0)
    per = rows_ref.shape[1] // BLOCK
    in_order = lax.broadcasted_iota(jnp.int32, (1, BLOCK), 1)
    for b in range(per):
        row = place_ref[1] + step * per + b
        within = jnp.bitwise_and(ids_ref[pl.ds(row, 1), :], BLOCK - 1)
        within = jnp.where(place_ref[0] == 0, within, in_order)
        columns = slice(b * BLOCK, (b + 1) * BLOCK)
        rows_ref[:, columns] = dot(moved_ref[:, columns], selector(within)).astype(jnp.bfloat16)
    pre_ref[...] = dot(weight_ref[0], rows_ref[...]) + bias_ref[...]


def arrived(place, ids, moved, weights, bias):
    features, owned = moved.shape
    hidden = weights.shape[1]
    wide = 2 * BLOCK
    return pl.pallas_call(
        arrived_kernel,
        grid_spec=pltpu.PrefetchScalarGridSpec(
            num_scalar_prefetch=1,
            grid=(owned // wide,),
            in_specs=[
                pl.BlockSpec(memory_space=pltpu.VMEM),
                pl.BlockSpec((features, wide), lambda i, place: (0, i)),
                pl.BlockSpec((1, hidden, features), lambda i, place: (place[0], 0, 0)),
                pl.BlockSpec(memory_space=pltpu.VMEM),
            ],
            out_specs=[
                pl.BlockSpec((features, wide), lambda i, place: (0, i)),
                pl.BlockSpec((hidden, wide), lambda i, place: (0, i)),
            ],
        ),
        out_shape=[
            jax.ShapeDtypeStruct((features, owned), jnp.bfloat16),
            jax.ShapeDtypeStruct((hidden, owned), jnp.float32),
        ],
        compiler_params=pltpu.CompilerParams(vmem_limit_bytes=24 * MIB),
        cost_estimate=pl.CostEstimate(flops=2_000_000_000, bytes_accessed=6 * MIB, transcendentals=0),
        name="first_arrived",
    )(place, ids, moved, weights, bias)


def gelu_and_slope(pre):
    c, k = 0.7978845608028654, 0.044715
    square = pre * pre
    t = jnp.tanh(c * pre * (1.0 + k * square))
    half = 0.5 * (1.0 + t)
    slope = half + 0.5 * pre * (1.0 - t * t) * (c * (1.0 + 3.0 * k * square))
    return pre * half, slope


def finish_kernel(
    place_ref, pre_hbm, second_hbm, first_hbm, weights_hbm, upstream_hbm, hidden_hbm, keep_hbm, send_hbm,
    pre_ref, second_ref, first_ref, weight_ref, upstream_ref, slope, hidden_ref, keep_ref, send_ref, load, leave,
):
    owned = pre_ref.shape[1]
    wide = 2 * BLOCK
    core, limit = place_ref[0], place_ref[2]

    load_weight = pltpu.make_async_copy(weights_hbm.at[1 - core], weight_ref, load.at[0])
    load_first = pltpu.make_async_copy(first_hbm, first_ref, load.at[1])
    halves = []
    for h in range(2):
        columns = slice(h * owned // 2, (h + 1) * owned // 2)
        pairs = ((second_hbm, second_ref), (pre_hbm, pre_ref), (upstream_hbm, upstream_ref))
        halves.append(
            [
                pltpu.make_async_copy(source.at[:, columns], target.at[:, columns], load.at[2 + 3 * h + k])
                for k, (source, target) in enumerate(pairs)
            ]
        )
    load_weight.start()
    for copy in halves[0] + halves[1] + [load_first]:
        copy.start()
    load_weight.wait()

    for h in range(2):
        for copy in halves[h]:
            copy.wait()
        for j in range(h * owned // 2, (h + 1) * owned // 2, wide):
            columns = slice(j, j + wide)
            active, back = gelu_and_slope(dot(weight_ref[...], second_ref[:, columns]) + pre_ref[:, columns])
            positions = j + lax.broadcasted_iota(jnp.int32, (1, wide), 1)
            valid = jnp.where(positions < limit, 1.0, 0.0)
            hidden_ref[:, columns] = (active * valid).astype(jnp.bfloat16)
            slope[:, columns] = (upstream_ref[:, columns].astype(jnp.float32) * back * valid).astype(jnp.bfloat16)
    leave_hidden = pltpu.make_async_copy(hidden_ref, hidden_hbm, leave.at[0])
    leave_hidden.start()

    owners, share, _ = keep_ref.shape
    group = 4

    def grads(left_ref, out_ref):
        for i in range(0, owners, group):
            total = dot(left_ref[i * share : (i + group) * share, :], slope[...], NT)
            out_ref[i : i + group] = total.reshape(group, share, -1).astype(out_ref.dtype)

    grads(second_ref, send_ref)
    leave_send = pltpu.make_async_copy(send_ref, send_hbm, leave.at[1])
    leave_send.start()
    load_first.wait()
    grads(first_ref, keep_ref)
    leave_keep = pltpu.make_async_copy(keep_ref, keep_hbm, leave.at[2])
    leave_keep.start()
    leave_hidden.wait()
    leave_send.wait()
    leave_keep.wait()


def finish(place, pre, second, first, weights, upstream, owners):
    hidden, owned = pre.shape
    features = second.shape[0]
    part = (owners, features // owners, hidden)
    anywhere = pl.BlockSpec(memory_space=pl.ANY)
    outs = [
        jax.ShapeDtypeStruct((hidden, owned), jnp.bfloat16),
        jax.ShapeDtypeStruct(part, jnp.float32),
        jax.ShapeDtypeStruct(part, jnp.bfloat16),
    ]
    return pl.pallas_call(
        finish_kernel,
        in_specs=[pl.BlockSpec(memory_space=pltpu.SMEM)] + [anywhere] * 5,
        out_specs=[anywhere] * 3,
        out_shape=outs,
        scratch_shapes=[pltpu.VMEM(a.shape, a.dtype) for a in (pre, second, first, weights[0], upstream)]
        + [pltpu.VMEM((hidden, owned), jnp.bfloat16)]
        + [pltpu.VMEM(a.shape, a.dtype) for a in outs]
        + [pltpu.SemaphoreType.DMA((8,)), pltpu.SemaphoreType.DMA((3,))],
        compiler_params=pltpu.CompilerParams(vmem_limit_bytes=WHOLE),
        cost_estimate=pl.CostEstimate(flops=2_000_000_000, bytes_accessed=9 * MIB, transcendentals=262144),
        name="finish",
    )(place, pre, second, first, weights, upstream)


def on_device(
    node_table, node_ids, block_lists, block_counts, tiles, batch_sizes, w_self, w_neigh, bias, cotangent
):
    owners = lax.axis_size(FEAT)
    rank, core = lax.axis_index(FEAT), lax.axis_index("core")
    table = jnp.swapaxes(node_table[0], 0, 1)
    width = table.shape[0]
    ids = node_ids[0].reshape(-1, BLOCK)
    owned = cotangent.shape[1]

    lists = jnp.transpose(block_lists, (2, 0, 1))
    place = jnp.stack([core, rank * (owned // BLOCK), batch_sizes[0] - rank * owned])
    operands = (core.reshape(1), lists, block_counts, ids, table, tiles[0], owners)
    weights = jnp.stack([w_self.T, w_neigh.T])

    first = outgoing(first_kernel, *operands, "first_outgoing")
    moved = lax.all_to_all(first, FEAT, split_axis=0, concat_axis=0, tiled=True)
    second = outgoing(second_kernel, *operands, "second_outgoing")
    second = lax.all_to_all(second, FEAT, split_axis=0, concat_axis=0, tiled=True)
    first, pre = arrived(place, ids, moved.reshape(-1, owned), weights, bias[:, None])
    second = second.reshape(-1, owned)
    hidden, keep, send = finish(place, pre, second, first, weights, cotangent[0].T, owners)

    got = lax.ppermute(send, "core", [(0, 1), (1, 0)])
    parts = lax.all_to_all((keep + got).astype(jnp.bfloat16), FEAT, split_axis=0, concat_axis=0, tiled=True)
    part = jnp.sum(parts, axis=0, dtype=jnp.float32).astype(jnp.bfloat16)
    copies = jnp.broadcast_to(part[None], (lax.axis_size(GRP), *part.shape))
    terms = lax.all_to_all(copies, GRP, split_axis=0, concat_axis=0, tiled=True)
    terms = terms.reshape(-1, lax.axis_size("core"), *part.shape)
    total = jnp.sum(terms, axis=0, dtype=jnp.float32)
    return (hidden.T[None], total[0], total[1])


def solution(mesh):
    axes = Mesh(mesh.devices.reshape(4, 4, 4, 2), ("z", "y", "x", "core"))
    in_specs = (
        P(GRP, None, FEAT),
        P(GRP, None),
        P(GRP, None, None),
        P(GRP, None),
        P(GRP, None, None, None, None),
        P(GRP),
        P(),
        P(),
        P(),
        P(GRP, FEAT, None),
    )
    out_specs = (P(GRP, FEAT, None), P(FEAT, None), P(FEAT, None))
    return jax.shard_map(on_device, mesh=axes, in_specs=in_specs, out_specs=out_specs, check_vma=False)
```

```python
import jax
import jax.numpy as jnp
from jax import lax
from jax.experimental import pallas as pl
from jax.experimental.pallas import tpu as pltpu
from jax.sharding import Mesh, PartitionSpec as P

BLOCK = 128
MIB = 1 << 20
WHOLE = 60 * MIB
FEAT = ("z", "y")
GRP = ("x", "core")
NT = (((1,), (1,)), ((), ()))
NN = (((1,), (0,)), ((), ()))


def dot(left, right, dims=NN):
    return lax.dot_general(left, right, dims, preferred_element_type=jnp.float32)


def selector(within):
    rows = lax.broadcasted_iota(jnp.int32, (BLOCK, BLOCK), 0)
    return jnp.where(rows == within, 1.0, 0.0).astype(jnp.bfloat16)


def read_blocks(ids_ref, vector, which, sem):
    lanes = lax.broadcasted_iota(jnp.int32, (vector.shape[0], BLOCK), 1)
    first = jnp.where(lanes == 0, 1.0, 0.0).astype(jnp.bfloat16)
    blocks = lax.shift_right_logical(ids_ref[...], 7).astype(jnp.float32).astype(jnp.bfloat16)
    vector[...] = dot(first, blocks, NT).astype(jnp.int32)
    copy = pltpu.make_async_copy(vector, which, sem)
    copy.start()
    copy.wait()


def block_of(table, w):
    return table[:, pl.ds(pl.multiple_of(w * BLOCK, BLOCK), BLOCK)]


def in_run_order(chosen, ids_row):
    within = jnp.broadcast_to(jnp.bitwise_and(ids_row, BLOCK - 1), (8, BLOCK))
    chosen = chosen.astype(jnp.float32)
    rows = [jnp.take_along_axis(chosen[i : i + 8], within, axis=1) for i in range(0, chosen.shape[0], 8)]
    return jnp.concatenate(rows, axis=0).astype(jnp.bfloat16)


def outgoing_kernel(
    batch_ref, lists_ref, counts_ref, ids_ref, table_hbm, tiles_hbm, out_hbm, size_ref, rows, table, tiles, vector, which, load, leave
):
    blocks = ids_ref.shape[0]
    owners, width, owned = rows.shape
    width = width // 2
    per = owned // BLOCK
    slots, dst_blocks = lists_ref.shape[0], lists_ref.shape[2]
    together = 4

    def load_tiles(r):
        part = pl.ds(r * per, per)
        return pltpu.make_async_copy(tiles_hbm.at[part], tiles.at[part], load.at[r])

    known = table.at[:, pl.ds(0, table_hbm.shape[1])]
    load_table = pltpu.make_async_copy(table_hbm, known, load.at[owners + 1])
    load_table.start()
    for r in range(together):
        load_tiles(r).start()
    size_ref[...] = jnp.full(size_ref.shape, batch_ref[0], jnp.int32)
    table[:, table_hbm.shape[1] :] = jnp.zeros((width, BLOCK), table.dtype)
    read_blocks(ids_ref, vector, which, load.at[owners])
    load_table.wait()
    for r in range(together, owners):
        load_tiles(r).start()

    def aggregated(d):
        count = counts_ref[0, d]
        left = []
        for s in range(slots):
            used = s < count
            n = lists_ref[s, 0, d]
            w = jnp.where(used, which[0, n], blocks)
            source = in_run_order(block_of(table, w), ids_ref[pl.ds(n, 1), :])
            ones = jnp.full((16, BLOCK), jnp.where(used, 1.0, 0.0), jnp.float32).astype(jnp.bfloat16)
            left.append(jnp.concatenate([source, ones], axis=0))
        right = jnp.concatenate([tiles[d, s] for s in range(slots)], axis=1)
        total = dot(jnp.concatenate(left, axis=1), right, NT)
        return (total[:width] * (1.0 / total[width : width + 1])).astype(jnp.bfloat16)

    def some(i, carry):
        for k in range(together):
            load_tiles(i * together + k).wait()
        first = i * together * per
        results = [aggregated(first + k) for k in range(together * per)]
        own = [block_of(table, which[0, first + k]) for k in range(together * per)]
        for k in range(together * per):
            r, columns = i * together + k // per, slice((k % per) * BLOCK, (k % per + 1) * BLOCK)
            rows[r, :width, columns] = own[k]
            rows[r, width:, columns] = results[k]
        for k in range(together):
            r = i * together + k
            pltpu.make_async_copy(rows.at[r], out_hbm.at[r], leave.at[r]).start()
        return carry

    lax.fori_loop(0, dst_blocks // per // together, some, 0)
    for r in range(owners):
        pltpu.make_async_copy(rows.at[r], out_hbm.at[r], leave.at[r]).wait()


def outgoing(batch, lists, counts, ids, table, tiles, owners):
    width, rows = table.shape
    blocks = rows // BLOCK
    smem, vmem = pl.BlockSpec(memory_space=pltpu.SMEM), pl.BlockSpec(memory_space=pltpu.VMEM)
    anywhere = pl.BlockSpec(memory_space=pl.ANY)
    out = (owners, 2 * width, tiles.shape[0] // owners * BLOCK)
    return pl.pallas_call(
        outgoing_kernel,
        in_specs=[smem, smem, smem, vmem, anywhere, anywhere],
        out_specs=[anywhere, vmem],
        out_shape=[jax.ShapeDtypeStruct(out, jnp.bfloat16), jax.ShapeDtypeStruct((8, BLOCK), jnp.int32)],
        scratch_shapes=[
            pltpu.VMEM(out, jnp.bfloat16),
            pltpu.VMEM((width, rows + BLOCK), jnp.bfloat16),
            pltpu.VMEM(tiles.shape, jnp.bfloat16),
            pltpu.VMEM((8, blocks), jnp.int32),
            pltpu.SMEM((8, blocks), jnp.int32),
            pltpu.SemaphoreType.DMA((owners + 2,)),
            pltpu.SemaphoreType.DMA((owners,)),
        ],
        compiler_params=pltpu.CompilerParams(vmem_limit_bytes=WHOLE),
        cost_estimate=pl.CostEstimate(flops=4_000_000_000, bytes_accessed=20 * MIB, transcendentals=0),
        name="pick_and_aggregate",
    )(batch, lists, counts, ids, table, tiles)


def gelu_and_slope(pre):
    c, k = 0.7978845608028654, 0.044715
    square = pre * pre
    t = jnp.tanh(c * pre * (1.0 + k * square))
    half = 0.5 * (1.0 + t)
    slope = half + 0.5 * pre * (1.0 - t * t) * (c * (1.0 + 3.0 * k * square))
    return pre * half, slope


def move_lanes(rows, order):
    order = jnp.broadcast_to(order, (8, BLOCK))
    moved = [jnp.take_along_axis(rows[i : i + 8], order, axis=1) for i in range(0, rows.shape[0], 8)]
    return jnp.concatenate(moved, axis=0)


def finish_kernel(
    size_ref, bias_ref, ids_hbm, moved_hbm, self_hbm, neigh_hbm, upstream_hbm, hidden_hbm, keep_hbm, send_hbm,
    ids_ref, rows, weights, turned, upstream_ref, slopes, hidden_ref, keep_ref, send_ref, load, leave,
):
    owners, share, owned = rows.shape[1:]
    features = owners * share
    per = owned // BLOCK
    rank, core = lax.axis_index(FEAT), lax.axis_index("core")
    own_slot, agg_slot = core, 1 - core

    load_ids = pltpu.make_async_copy(ids_hbm.at[pl.ds(pl.multiple_of(rank * per, per), per)], ids_ref, load.at[0])
    load_weights = [
        pltpu.make_async_copy(source, weights.at[k], load.at[1 + k]) for k, source in enumerate((self_hbm, neigh_hbm))
    ]
    load_upstream = pltpu.make_async_copy(upstream_hbm, upstream_ref, load.at[3])
    half = owned // 2
    load_rows = []
    for h in range(2):
        columns = slice(h * half, (h + 1) * half)
        for k, slot in enumerate((own_slot, agg_slot)):
            load_rows.append(
                pltpu.make_async_copy(
                    moved_hbm.at[:, k * share : (k + 1) * share, columns],
                    rows.at[slot, :, :, columns],
                    load.at[4 + 2 * h + k],
                )
            )
    for copy in [load_ids] + load_weights + load_rows[:2] + [load_upstream] + load_rows[2:]:
        copy.start()

    limit = size_ref[:1, :] - rank * owned
    load_ids.wait()
    lanes = lax.broadcasted_iota(jnp.int32, (8, BLOCK), 1).astype(jnp.bfloat16)
    orders = [jnp.bitwise_and(ids_ref[b : b + 1, :], BLOCK - 1) for b in range(per)]
    inverse = [dot(lanes, selector(order), NT).astype(jnp.int32) for order in orders]
    offset = jnp.broadcast_to(bias_ref[...], (BLOCK, bias_ref.shape[1])).T
    for k in range(2):
        load_weights[k].wait()
        turned[k] = weights[k].T

    def rows_of(slot, columns):
        return rows[slot, :, :, columns].reshape(features, BLOCK)

    for h in range(2):
        load_rows[2 * h].wait()
        load_rows[2 * h + 1].wait()
        if h == 0:
            load_upstream.wait()
        for b in range(h * per // 2, (h + 1) * per // 2):
            columns = slice(b * BLOCK, (b + 1) * BLOCK)
            own = move_lanes(dot(turned[0], rows_of(own_slot, columns)), orders[b])
            pre = own + dot(turned[1], rows_of(agg_slot, columns)) + offset
            active, back = gelu_and_slope(pre)
            positions = b * BLOCK + lax.broadcasted_iota(jnp.int32, (1, BLOCK), 1)
            valid = jnp.where(positions < limit, 1.0, 0.0)
            hidden_ref[:, columns] = (active * valid).astype(jnp.bfloat16)
            upstream = upstream_ref[columns, :].astype(jnp.float32).T
            slope = (upstream * back * valid).astype(jnp.bfloat16)
            slopes[agg_slot, :, columns] = slope
            slopes[own_slot, :, columns] = move_lanes(slope.astype(jnp.float32), inverse[b]).astype(jnp.bfloat16)
    leave_hidden = pltpu.make_async_copy(hidden_ref, hidden_hbm, leave.at[0])
    leave_hidden.start()

    group = 4

    def grads(slot, out_ref):
        for i in range(0, owners, group):
            left = rows[slot, i : i + group].reshape(group * share, owned)
            total = dot(left, slopes[slot], NT)
            out_ref[i : i + group] = total.reshape(group, share, -1).astype(out_ref.dtype)

    grads(1, send_ref)
    leave_send = pltpu.make_async_copy(send_ref, send_hbm, leave.at[1])
    leave_send.start()
    grads(0, keep_ref)
    leave_keep = pltpu.make_async_copy(keep_ref, keep_hbm, leave.at[2])
    leave_keep.start()
    leave_hidden.wait()
    leave_send.wait()
    leave_keep.wait()


def finish(size, bias, ids, moved, w_self, w_neigh, upstream):
    owners, share, owned = moved.shape[0], moved.shape[1] // 2, moved.shape[2]
    features, hidden = w_self.shape
    part = (owners, share, hidden)
    vmem, anywhere = pl.BlockSpec(memory_space=pltpu.VMEM), pl.BlockSpec(memory_space=pl.ANY)
    outs = [
        jax.ShapeDtypeStruct((hidden, owned), jnp.bfloat16),
        jax.ShapeDtypeStruct(part, jnp.float32),
        jax.ShapeDtypeStruct(part, jnp.bfloat16),
    ]
    return pl.pallas_call(
        finish_kernel,
        in_specs=[vmem, vmem] + [anywhere] * 5,
        out_specs=[anywhere] * 3,
        out_shape=outs,
        scratch_shapes=[
            pltpu.VMEM((owned // BLOCK, BLOCK), jnp.int32),
            pltpu.VMEM((2, owners, share, owned), jnp.bfloat16),
            pltpu.VMEM((2, features, hidden), jnp.bfloat16),
            pltpu.VMEM((2, hidden, features), jnp.bfloat16),
            pltpu.VMEM(upstream.shape, jnp.bfloat16),
            pltpu.VMEM((2, hidden, owned), jnp.bfloat16),
        ]
        + [pltpu.VMEM(a.shape, a.dtype) for a in outs]
        + [pltpu.SemaphoreType.DMA((8,)), pltpu.SemaphoreType.DMA((3,))],
        compiler_params=pltpu.CompilerParams(vmem_limit_bytes=WHOLE),
        cost_estimate=pl.CostEstimate(flops=2_000_000_000, bytes_accessed=9 * MIB, transcendentals=262144),
        name="finish",
    )(size, bias, ids, moved, w_self, w_neigh, upstream)


def on_device(
    node_table, node_ids, block_lists, block_counts, tiles, batch_sizes, w_self, w_neigh, bias, cotangent
):
    owners = lax.axis_size(FEAT)
    core = lax.axis_index("core")
    table = jnp.swapaxes(node_table[0], 0, 1)
    ids = node_ids[0].reshape(-1, BLOCK)

    lists = jnp.transpose(block_lists, (2, 0, 1))
    rows, size = outgoing(batch_sizes, lists, block_counts, ids, table, tiles[0], owners)
    moved = lax.all_to_all(rows, FEAT, split_axis=0, concat_axis=0, tiled=True)
    hidden, keep, send = finish(size, bias[None], ids, moved, w_self, w_neigh, cotangent[0])

    got = lax.ppermute(send, "core", [(0, 1), (1, 0)])
    parts = lax.all_to_all((keep + got).astype(jnp.bfloat16), FEAT, split_axis=0, concat_axis=0, tiled=True)
    total = jnp.sum(parts, axis=0, dtype=jnp.float32)
    others = [lax.ppermute(total, "x", [(i, (i + k) % 4) for i in range(4)]) for k in (3, 1, 2)]
    total = (total + others[2]) + (others[0] + others[1])
    other = lax.ppermute(total, "core", [(0, 1), (1, 0)])
    first_core = core == 0
    return (
        hidden.T[None],
        jnp.where(first_core, total, other),
        jnp.where(first_core, other, total),
    )


def solution(mesh):
    axes = Mesh(mesh.devices.reshape(4, 4, 4, 2), ("z", "y", "x", "core"))
    in_specs = (
        P(GRP, None, FEAT),
        P(GRP, None),
        P(GRP, None, None),
        P(GRP, None),
        P(GRP, None, None, None, None),
        P(GRP),
        P(),
        P(),
        P(),
        P(GRP, FEAT, None),
    )
    out_specs = (P(GRP, FEAT, None), P(FEAT, None), P(FEAT, None))
    return jax.shard_map(on_device, mesh=axes, in_specs=in_specs, out_specs=out_specs, check_vma=False)
```

```python
import jax
import jax.numpy as jnp
from jax import lax
from jax.experimental import pallas as pl
from jax.experimental.pallas import tpu as pltpu
from jax.sharding import Mesh, PartitionSpec as P

BLOCK = 128
MIB = 1 << 20
WHOLE = 60 * MIB
FEAT = ("z", "y")
GRP = ("x", "core")
NT = (((1,), (1,)), ((), ()))
NN = (((1,), (0,)), ((), ()))


def dot(left, right, dims=NN):
    return lax.dot_general(left, right, dims, preferred_element_type=jnp.float32)


def selector(within):
    rows = lax.broadcasted_iota(jnp.int32, (BLOCK, BLOCK), 0)
    return jnp.where(rows == within, 1.0, 0.0).astype(jnp.bfloat16)


def read_blocks(ids_ref, vector, which, sem):
    lanes = lax.broadcasted_iota(jnp.int32, (vector.shape[0], BLOCK), 1)
    first = jnp.where(lanes == 0, 1.0, 0.0).astype(jnp.bfloat16)
    blocks = lax.shift_right_logical(ids_ref[...], 7).astype(jnp.float32).astype(jnp.bfloat16)
    vector[...] = dot(first, blocks, NT).astype(jnp.int32)
    copy = pltpu.make_async_copy(vector, which, sem)
    copy.start()
    copy.wait()


def block_of(table, w):
    return table[:, pl.ds(pl.multiple_of(w * BLOCK, BLOCK), BLOCK)]


def in_run_order(chosen, ids_row):
    within = jnp.broadcast_to(jnp.bitwise_and(ids_row, BLOCK - 1), (8, BLOCK))
    chosen = chosen.astype(jnp.float32)
    rows = [jnp.take_along_axis(chosen[i : i + 8], within, axis=1) for i in range(0, chosen.shape[0], 8)]
    return jnp.concatenate(rows, axis=0).astype(jnp.bfloat16)


def outgoing_kernel(
    batch_ref, lists_ref, counts_ref, ids_ref, table_hbm, tiles_hbm, out_hbm, size_ref, rows, table, tiles, vector, which, load, leave
):
    blocks = ids_ref.shape[0]
    owners, width, owned = rows.shape
    width = width // 2
    per = owned // BLOCK
    slots, dst_blocks = lists_ref.shape[0], lists_ref.shape[2]
    together = 4

    def load_tiles(r):
        part = pl.ds(r * per, per)
        return pltpu.make_async_copy(tiles_hbm.at[part], tiles.at[part], load.at[r])

    known = table.at[:, pl.ds(0, table_hbm.shape[1])]
    load_table = pltpu.make_async_copy(table_hbm, known, load.at[owners + 1])
    load_table.start()
    for r in range(together):
        load_tiles(r).start()
    size_ref[...] = jnp.full(size_ref.shape, batch_ref[0], jnp.int32)
    table[:, table_hbm.shape[1] :] = jnp.zeros((width, BLOCK), table.dtype)
    read_blocks(ids_ref, vector, which, load.at[owners])
    load_table.wait()
    for r in range(together, owners):
        load_tiles(r).start()

    def aggregated(d):
        count = counts_ref[0, d]
        left = []
        for s in range(slots):
            used = s < count
            n = lists_ref[s, 0, d]
            w = jnp.where(used, which[0, n], blocks)
            source = in_run_order(block_of(table, w), ids_ref[pl.ds(n, 1), :])
            ones = jnp.full((16, BLOCK), jnp.where(used, 1.0, 0.0), jnp.float32).astype(jnp.bfloat16)
            left.append(jnp.concatenate([source, ones], axis=0))
        right = jnp.concatenate([tiles[d, s] for s in range(slots)], axis=1)
        total = dot(jnp.concatenate(left, axis=1), right, NT)
        return (total[:width] * (1.0 / total[width : width + 1])).astype(jnp.bfloat16)

    def some(i, carry):
        for k in range(together):
            load_tiles(i * together + k).wait()
        first = i * together * per
        results = [aggregated(first + k) for k in range(together * per)]
        own = [block_of(table, which[0, first + k]) for k in range(together * per)]
        for k in range(together * per):
            r, columns = i * together + k // per, slice((k % per) * BLOCK, (k % per + 1) * BLOCK)
            rows[r, :width, columns] = own[k]
            rows[r, width:, columns] = results[k]
        for k in range(together):
            r = i * together + k
            pltpu.make_async_copy(rows.at[r], out_hbm.at[r], leave.at[r]).start()
        return carry

    lax.fori_loop(0, dst_blocks // per // together, some, 0)
    for r in range(owners):
        pltpu.make_async_copy(rows.at[r], out_hbm.at[r], leave.at[r]).wait()


def outgoing(batch, lists, counts, ids, table, tiles, owners):
    width, rows = table.shape
    blocks = rows // BLOCK
    smem, vmem = pl.BlockSpec(memory_space=pltpu.SMEM), pl.BlockSpec(memory_space=pltpu.VMEM)
    anywhere = pl.BlockSpec(memory_space=pl.ANY)
    out = (owners, 2 * width, tiles.shape[0] // owners * BLOCK)
    return pl.pallas_call(
        outgoing_kernel,
        in_specs=[smem, smem, smem, vmem, anywhere, anywhere],
        out_specs=[anywhere, vmem],
        out_shape=[jax.ShapeDtypeStruct(out, jnp.bfloat16), jax.ShapeDtypeStruct((8, BLOCK), jnp.int32)],
        scratch_shapes=[
            pltpu.VMEM(out, jnp.bfloat16),
            pltpu.VMEM((width, rows + BLOCK), jnp.bfloat16),
            pltpu.VMEM(tiles.shape, jnp.bfloat16),
            pltpu.VMEM((8, blocks), jnp.int32),
            pltpu.SMEM((8, blocks), jnp.int32),
            pltpu.SemaphoreType.DMA((owners + 2,)),
            pltpu.SemaphoreType.DMA((owners,)),
        ],
        compiler_params=pltpu.CompilerParams(vmem_limit_bytes=WHOLE),
        cost_estimate=pl.CostEstimate(flops=4_000_000_000, bytes_accessed=20 * MIB, transcendentals=0),
        name="pick_and_aggregate",
    )(batch, lists, counts, ids, table, tiles)


def gelu_and_slope(pre):
    c, k = 0.7978845608028654, 0.044715
    square = pre * pre
    t = jnp.tanh(c * pre * (1.0 + k * square))
    half = 0.5 * (1.0 + t)
    slope = half + 0.5 * pre * (1.0 - t * t) * (c * (1.0 + 3.0 * k * square))
    return pre * half, slope


def move_lanes(rows, order):
    order = jnp.broadcast_to(order, (8, BLOCK))
    moved = [jnp.take_along_axis(rows[i : i + 8], order, axis=1) for i in range(0, rows.shape[0], 8)]
    return jnp.concatenate(moved, axis=0)


def finish_kernel(
    size_ref, bias_ref, ids_ref, moved_ref, self_ref, neigh_ref, upstream_ref, hidden_ref, keep_ref, send_ref,
    turned, slopes,
):
    owners, share, hidden = keep_ref.shape
    owned = moved_ref.shape[2]
    features = owners * share
    per = owned // BLOCK
    rank, core = lax.axis_index(FEAT), lax.axis_index("core")
    limit = size_ref[:1, :] - rank * owned

    lanes = lax.broadcasted_iota(jnp.int32, (8, BLOCK), 1).astype(jnp.bfloat16)
    mine = ids_ref[pl.ds(pl.multiple_of(rank * per, per), per), :]
    orders = [jnp.bitwise_and(mine[b : b + 1, :], BLOCK - 1) for b in range(per)]
    inverse = [dot(lanes, selector(order), NT).astype(jnp.int32) for order in orders]
    offset = jnp.broadcast_to(bias_ref[...], (BLOCK, hidden)).T
    turned[0] = self_ref[...].T
    turned[1] = neigh_ref[...].T

    for b in range(per):
        columns = slice(b * BLOCK, (b + 1) * BLOCK)
        own = dot(turned[0], moved_ref[:, :share, columns].reshape(features, BLOCK))
        pre = move_lanes(own, orders[b]) + offset
        pre = pre + dot(turned[1], moved_ref[:, share:, columns].reshape(features, BLOCK))
        active, back = gelu_and_slope(pre)
        positions = b * BLOCK + lax.broadcasted_iota(jnp.int32, (1, BLOCK), 1)
        valid = jnp.where(positions < limit, 1.0, 0.0)
        hidden_ref[:, columns] = (active * valid).astype(jnp.bfloat16)
        upstream = upstream_ref[columns, :].astype(jnp.float32).T
        slope = (upstream * back * valid).astype(jnp.bfloat16)
        slopes[1, :, columns] = slope
        slopes[0, :, columns] = move_lanes(slope.astype(jnp.float32), inverse[b]).astype(jnp.bfloat16)

    group = 4

    def grads(k, out_ref):
        start = pl.multiple_of(k * share, share)
        for i in range(0, owners, group):
            left = moved_ref[i : i + group, pl.ds(start, share), :].reshape(group * share, owned)
            out_ref[i : i + group] = dot(left, slopes[k], NT).reshape(group, share, hidden).astype(out_ref.dtype)

    grads(1 - core, send_ref)
    grads(core, keep_ref)


def finish(size, bias, ids, moved, w_self, w_neigh, upstream):
    owners, share, owned = moved.shape[0], moved.shape[1] // 2, moved.shape[2]
    features, hidden = w_self.shape
    part = (owners, share, hidden)
    vmem = pl.BlockSpec(memory_space=pltpu.VMEM)
    return pl.pallas_call(
        finish_kernel,
        in_specs=[vmem] * 7,
        out_specs=[vmem] * 3,
        out_shape=[
            jax.ShapeDtypeStruct((hidden, owned), jnp.bfloat16),
            jax.ShapeDtypeStruct(part, jnp.float32),
            jax.ShapeDtypeStruct(part, jnp.bfloat16),
        ],
        scratch_shapes=[
            pltpu.VMEM((2, hidden, features), jnp.bfloat16),
            pltpu.VMEM((2, hidden, owned), jnp.bfloat16),
        ],
        compiler_params=pltpu.CompilerParams(vmem_limit_bytes=24 * MIB),
        cost_estimate=pl.CostEstimate(flops=2_000_000_000, bytes_accessed=9 * MIB, transcendentals=262144),
        name="finish",
    )(size, bias, ids, moved, w_self, w_neigh, upstream)


def on_device(
    node_table, node_ids, block_lists, block_counts, tiles, batch_sizes, w_self, w_neigh, bias, cotangent
):
    owners = lax.axis_size(FEAT)
    core = lax.axis_index("core")
    table = jnp.swapaxes(node_table[0], 0, 1)
    ids = node_ids[0].reshape(-1, BLOCK)

    lists = jnp.transpose(block_lists, (2, 0, 1))
    rows, size = outgoing(batch_sizes, lists, block_counts, ids, table, tiles[0], owners)
    moved = lax.all_to_all(rows, FEAT, split_axis=0, concat_axis=0, tiled=True)
    hidden, keep, send = finish(size, bias[None], ids, moved, w_self, w_neigh, cotangent[0])

    got = lax.ppermute(send, "core", [(0, 1), (1, 0)])
    parts = lax.all_to_all((keep + got).astype(jnp.bfloat16), FEAT, split_axis=0, concat_axis=0, tiled=True)
    total = jnp.sum(parts, axis=0, dtype=jnp.float32)
    others = [lax.ppermute(total, "x", [(i, (i + k) % 4) for i in range(4)]) for k in (3, 1, 2)]
    total = (total + others[2]) + (others[0] + others[1])
    other = lax.ppermute(total, "core", [(0, 1), (1, 0)])
    first_core = core == 0
    return (
        hidden.T[None],
        jnp.where(first_core, total, other),
        jnp.where(first_core, other, total),
    )


def solution(mesh):
    axes = Mesh(mesh.devices.reshape(4, 4, 4, 2), ("z", "y", "x", "core"))
    in_specs = (
        P(GRP, None, FEAT),
        P(GRP, None),
        P(GRP, None, None),
        P(GRP, None),
        P(GRP, None, None, None, None),
        P(GRP),
        P(),
        P(),
        P(),
        P(GRP, FEAT, None),
    )
    out_specs = (P(GRP, FEAT, None), P(FEAT, None), P(FEAT, None))
    return jax.shard_map(on_device, mesh=axes, in_specs=in_specs, out_specs=out_specs, check_vma=False)
```

```python
import jax
import jax.numpy as jnp
from jax import lax
from jax.experimental import pallas as pl
from jax.experimental.pallas import tpu as pltpu
from jax.sharding import Mesh, PartitionSpec as P

BLOCK = 128
MIB = 1 << 20
WHOLE = 60 * MIB
FEAT = ("z", "y")
GRP = ("x", "core")
NT = (((1,), (1,)), ((), ()))
NN = (((1,), (0,)), ((), ()))


def dot(left, right, dims=NN):
    return lax.dot_general(left, right, dims, preferred_element_type=jnp.float32)


def selector(within):
    rows = lax.broadcasted_iota(jnp.int32, (BLOCK, BLOCK), 0)
    return jnp.where(rows == within, 1.0, 0.0).astype(jnp.bfloat16)


def read_blocks(ids_ref, vector, which, sem):
    lanes = lax.broadcasted_iota(jnp.int32, (vector.shape[0], BLOCK), 1)
    first = jnp.where(lanes == 0, 1.0, 0.0).astype(jnp.bfloat16)
    blocks = lax.shift_right_logical(ids_ref[...], 7).astype(jnp.float32).astype(jnp.bfloat16)
    vector[...] = dot(first, blocks, NT).astype(jnp.int32)
    copy = pltpu.make_async_copy(vector, which, sem)
    copy.start()
    copy.wait()


def block_of(table, w):
    return table[:, pl.ds(pl.multiple_of(w * BLOCK, BLOCK), BLOCK)]


def in_run_order(chosen, ids_row):
    within = jnp.broadcast_to(jnp.bitwise_and(ids_row, BLOCK - 1), (8, BLOCK))
    chosen = chosen.astype(jnp.float32)
    rows = [jnp.take_along_axis(chosen[i : i + 8], within, axis=1) for i in range(0, chosen.shape[0], 8)]
    return jnp.concatenate(rows, axis=0).astype(jnp.bfloat16)


def outgoing_kernel(
    batch_ref, lists_ref, counts_ref, ids_ref, table_hbm, tiles_hbm, out_hbm, size_ref, rows, table, tiles, vector, which, load, leave
):
    blocks = ids_ref.shape[0]
    owners, width, owned = rows.shape
    width = width // 2
    per = owned // BLOCK
    slots, dst_blocks = lists_ref.shape[0], lists_ref.shape[2]
    together = 4

    def load_tiles(r):
        part = pl.ds(r * per, per)
        return pltpu.make_async_copy(tiles_hbm.at[part], tiles.at[part], load.at[r])

    known = table.at[:, pl.ds(0, table_hbm.shape[1])]
    load_table = pltpu.make_async_copy(table_hbm, known, load.at[owners + 1])
    load_table.start()
    for r in range(together):
        load_tiles(r).start()
    size_ref[...] = jnp.full(size_ref.shape, batch_ref[0], jnp.int32)
    table[:, table_hbm.shape[1] :] = jnp.zeros((width, BLOCK), table.dtype)
    read_blocks(ids_ref, vector, which, load.at[owners])
    load_table.wait()
    for r in range(together, owners):
        load_tiles(r).start()

    def aggregated(d):
        count = counts_ref[0, d]
        left = []
        for s in range(slots):
            used = s < count
            n = lists_ref[s, 0, d]
            w = jnp.where(used, which[0, n], blocks)
            source = in_run_order(block_of(table, w), ids_ref[pl.ds(n, 1), :])
            ones = jnp.full((16, BLOCK), jnp.where(used, 1.0, 0.0), jnp.float32).astype(jnp.bfloat16)
            left.append(jnp.concatenate([source, ones], axis=0))
        right = jnp.concatenate([tiles[d, s] for s in range(slots)], axis=1)
        total = dot(right, jnp.concatenate(left, axis=1), NT).T
        return (total[:width] * (1.0 / total[width : width + 1])).astype(jnp.bfloat16)

    def some(i, carry):
        for k in range(together):
            load_tiles(i * together + k).wait()
        first = i * together * per
        results = [aggregated(first + k) for k in range(together * per)]
        own = [block_of(table, which[0, first + k]) for k in range(together * per)]
        for k in range(together * per):
            r, columns = i * together + k // per, slice((k % per) * BLOCK, (k % per + 1) * BLOCK)
            rows[r, :width, columns] = own[k]
            rows[r, width:, columns] = results[k]
        for k in range(together):
            r = i * together + k
            pltpu.make_async_copy(rows.at[r], out_hbm.at[r], leave.at[r]).start()
        return carry

    lax.fori_loop(0, dst_blocks // per // together, some, 0)
    for r in range(owners):
        pltpu.make_async_copy(rows.at[r], out_hbm.at[r], leave.at[r]).wait()


def outgoing(batch, lists, counts, ids, table, tiles, owners):
    width, rows = table.shape
    blocks = rows // BLOCK
    smem, vmem = pl.BlockSpec(memory_space=pltpu.SMEM), pl.BlockSpec(memory_space=pltpu.VMEM)
    anywhere = pl.BlockSpec(memory_space=pl.ANY)
    out = (owners, 2 * width, tiles.shape[0] // owners * BLOCK)
    return pl.pallas_call(
        outgoing_kernel,
        in_specs=[smem, smem, smem, vmem, anywhere, anywhere],
        out_specs=[anywhere, vmem],
        out_shape=[jax.ShapeDtypeStruct(out, jnp.bfloat16), jax.ShapeDtypeStruct((8, BLOCK), jnp.int32)],
        scratch_shapes=[
            pltpu.VMEM(out, jnp.bfloat16),
            pltpu.VMEM((width, rows + BLOCK), jnp.bfloat16),
            pltpu.VMEM(tiles.shape, jnp.bfloat16),
            pltpu.VMEM((8, blocks), jnp.int32),
            pltpu.SMEM((8, blocks), jnp.int32),
            pltpu.SemaphoreType.DMA((owners + 2,)),
            pltpu.SemaphoreType.DMA((owners,)),
        ],
        compiler_params=pltpu.CompilerParams(vmem_limit_bytes=WHOLE),
        cost_estimate=pl.CostEstimate(flops=4_000_000_000, bytes_accessed=20 * MIB, transcendentals=0),
        name="pick_and_aggregate",
    )(batch, lists, counts, ids, table, tiles)


def gelu_and_slope(pre):
    c, k = 0.7978845608028654, 0.044715
    square = pre * pre
    t = jnp.tanh(c * pre * (1.0 + k * square))
    half = 0.5 * (1.0 + t)
    slope = half + 0.5 * pre * (1.0 - t * t) * (c * (1.0 + 3.0 * k * square))
    return pre * half, slope


def move_lanes(rows, order):
    order = jnp.broadcast_to(order, (8, BLOCK))
    moved = [jnp.take_along_axis(rows[i : i + 8], order, axis=1) for i in range(0, rows.shape[0], 8)]
    return jnp.concatenate(moved, axis=0)


def grads(k, moved_ref, slope, out_ref):
    owners, share, hidden = out_ref.shape
    start = pl.multiple_of(k * share, share)
    group = 4
    for i in range(0, owners, group):
        left = moved_ref[i : i + group, pl.ds(start, share), :].reshape(group * share, -1)
        out_ref[i : i + group] = dot(left, slope, NT).reshape(group, share, hidden).astype(out_ref.dtype)


def finish_kernel(
    size_ref, bias_ref, ids_ref, moved_ref, self_ref, neigh_ref, upstream_ref, hidden_ref, slope_ref, send_ref,
    turned, slopes,
):
    owners, share, hidden = send_ref.shape
    owned = moved_ref.shape[2]
    features = owners * share
    per = owned // BLOCK
    rank, core = lax.axis_index(FEAT), lax.axis_index("core")
    limit = size_ref[:1, :] - rank * owned

    lanes = lax.broadcasted_iota(jnp.int32, (8, BLOCK), 1).astype(jnp.bfloat16)
    mine = ids_ref[pl.ds(pl.multiple_of(rank * per, per), per), :]
    orders = [jnp.bitwise_and(mine[b : b + 1, :], BLOCK - 1) for b in range(per)]
    inverse = [dot(lanes, selector(order), NT).astype(jnp.int32) for order in orders]
    offset = jnp.broadcast_to(bias_ref[...], (BLOCK, hidden)).T
    turned[0] = self_ref[...].T
    turned[1] = neigh_ref[...].T

    for b in range(per):
        columns = slice(b * BLOCK, (b + 1) * BLOCK)
        own = dot(turned[0], moved_ref[:, :share, columns].reshape(features, BLOCK))
        pre = move_lanes(own, orders[b]) + offset
        pre = pre + dot(turned[1], moved_ref[:, share:, columns].reshape(features, BLOCK))
        active, back = gelu_and_slope(pre)
        positions = b * BLOCK + lax.broadcasted_iota(jnp.int32, (1, BLOCK), 1)
        valid = jnp.where(positions < limit, 1.0, 0.0)
        hidden_ref[:, columns] = (active * valid).astype(jnp.bfloat16)
        upstream = upstream_ref[columns, :].astype(jnp.float32).T
        slope = (upstream * back * valid).astype(jnp.bfloat16)
        slopes[1, :, columns] = slope
        slopes[0, :, columns] = move_lanes(slope.astype(jnp.float32), inverse[b]).astype(jnp.bfloat16)

    grads(1 - core, moved_ref, slopes[1 - core], send_ref)
    slope_ref[...] = slopes[core]


def keep_kernel(moved_ref, slope_ref, keep_ref):
    grads(lax.axis_index("core"), moved_ref, slope_ref[...], keep_ref)


def finish(size, bias, ids, moved, w_self, w_neigh, upstream):
    owners, share, owned = moved.shape[0], moved.shape[1] // 2, moved.shape[2]
    features, hidden = w_self.shape
    part = (owners, share, hidden)
    vmem = pl.BlockSpec(memory_space=pltpu.VMEM)
    return pl.pallas_call(
        finish_kernel,
        in_specs=[vmem] * 7,
        out_specs=[vmem] * 3,
        out_shape=[
            jax.ShapeDtypeStruct((hidden, owned), jnp.bfloat16),
            jax.ShapeDtypeStruct((hidden, owned), jnp.bfloat16),
            jax.ShapeDtypeStruct(part, jnp.bfloat16),
        ],
        scratch_shapes=[
            pltpu.VMEM((2, hidden, features), jnp.bfloat16),
            pltpu.VMEM((2, hidden, owned), jnp.bfloat16),
        ],
        compiler_params=pltpu.CompilerParams(vmem_limit_bytes=24 * MIB),
        cost_estimate=pl.CostEstimate(flops=2_000_000_000, bytes_accessed=9 * MIB, transcendentals=262144),
        name="finish",
    )(size, bias, ids, moved, w_self, w_neigh, upstream)


def keep_part(moved, slope):
    vmem = pl.BlockSpec(memory_space=pltpu.VMEM)
    part = (moved.shape[0], moved.shape[1] // 2, slope.shape[0])
    return pl.pallas_call(
        keep_kernel,
        in_specs=[vmem] * 2,
        out_specs=vmem,
        out_shape=jax.ShapeDtypeStruct(part, jnp.float32),
        compiler_params=pltpu.CompilerParams(vmem_limit_bytes=24 * MIB),
        cost_estimate=pl.CostEstimate(flops=1_000_000_000, bytes_accessed=4 * MIB, transcendentals=0),
        name="kept_gradient",
    )(moved, slope)


def on_device(
    node_table, node_ids, block_lists, block_counts, tiles, batch_sizes, w_self, w_neigh, bias, cotangent
):
    owners = lax.axis_size(FEAT)
    core = lax.axis_index("core")
    table = jnp.swapaxes(node_table[0], 0, 1)
    ids = node_ids[0].reshape(-1, BLOCK)

    lists = jnp.transpose(block_lists, (2, 0, 1))
    rows, size = outgoing(batch_sizes, lists, block_counts, ids, table, tiles[0], owners)
    moved = lax.all_to_all(rows, FEAT, split_axis=0, concat_axis=0, tiled=True)
    hidden, slope, send = finish(size, bias[None], ids, moved, w_self, w_neigh, cotangent[0])

    got = lax.ppermute(send, "core", [(0, 1), (1, 0)])
    keep = keep_part(moved, slope)
    parts = lax.all_to_all((keep + got).astype(jnp.bfloat16), FEAT, split_axis=0, concat_axis=0, tiled=True)
    total = jnp.sum(parts, axis=0, dtype=jnp.float32)
    others = [lax.ppermute(total, "x", [(i, (i + k) % 4) for i in range(4)]) for k in (3, 1, 2)]
    total = (total + others[2]) + (others[0] + others[1])
    other = lax.ppermute(total, "core", [(0, 1), (1, 0)])
    first_core = core == 0
    return (
        hidden.T[None],
        jnp.where(first_core, total, other),
        jnp.where(first_core, other, total),
    )


def solution(mesh):
    axes = Mesh(mesh.devices.reshape(4, 4, 4, 2), ("z", "y", "x", "core"))
    in_specs = (
        P(GRP, None, FEAT),
        P(GRP, None),
        P(GRP, None, None),
        P(GRP, None),
        P(GRP, None, None, None, None),
        P(GRP),
        P(),
        P(),
        P(),
        P(GRP, FEAT, None),
    )
    out_specs = (P(GRP, FEAT, None), P(FEAT, None), P(FEAT, None))
    return jax.shard_map(on_device, mesh=axes, in_specs=in_specs, out_specs=out_specs, check_vma=False)
```

```python
import jax
import jax.numpy as jnp
from jax import lax
from jax.experimental import pallas as pl
from jax.experimental.pallas import tpu as pltpu
from jax.sharding import Mesh, PartitionSpec as P

BLOCK = 128
MIB = 1 << 20
WHOLE = 60 * MIB
FEAT = ("z", "y")
GRP = ("x", "core")
NT = (((1,), (1,)), ((), ()))
NN = (((1,), (0,)), ((), ()))


def dot(left, right, dims=NN):
    return lax.dot_general(left, right, dims, preferred_element_type=jnp.float32)


def selector(within):
    rows = lax.broadcasted_iota(jnp.int32, (BLOCK, BLOCK), 0)
    return jnp.where(rows == within, 1.0, 0.0).astype(jnp.bfloat16)


def read_blocks(ids_ref, vector, which, sem):
    lanes = lax.broadcasted_iota(jnp.int32, (vector.shape[0], BLOCK), 1)
    first = jnp.where(lanes == 0, 1.0, 0.0).astype(jnp.bfloat16)
    blocks = lax.shift_right_logical(ids_ref[...], 7).astype(jnp.float32).astype(jnp.bfloat16)
    vector[...] = dot(first, blocks, NT).astype(jnp.int32)
    copy = pltpu.make_async_copy(vector, which, sem)
    copy.start()
    copy.wait()


def block_of(table, w):
    return table[:, pl.ds(pl.multiple_of(w * BLOCK, BLOCK), BLOCK)]


def in_run_order(chosen, ids_row):
    within = jnp.broadcast_to(jnp.bitwise_and(ids_row, BLOCK - 1), (8, BLOCK))
    chosen = chosen.astype(jnp.float32)
    rows = [jnp.take_along_axis(chosen[i : i + 8], within, axis=1) for i in range(0, chosen.shape[0], 8)]
    return jnp.concatenate(rows, axis=0).astype(jnp.bfloat16)


def outgoing_kernel(
    batch_ref, lists_ref, counts_ref, ids_ref, table_hbm, tiles_hbm, out_hbm, size_hbm, rows, size_ref, table, tiles, vector, which, load, leave
):
    blocks = ids_ref.shape[0]
    owners, width, owned = rows.shape
    width = width // 2
    per = owned // BLOCK
    slots, dst_blocks = lists_ref.shape[0], lists_ref.shape[2]
    together = 4

    def load_tiles(r):
        part = pl.ds(r * per, per)
        return pltpu.make_async_copy(tiles_hbm.at[part], tiles.at[part], load.at[r])

    known = table.at[:, pl.ds(0, table_hbm.shape[1])]
    load_table = pltpu.make_async_copy(table_hbm, known, load.at[owners + 1])
    load_table.start()
    for r in range(together):
        load_tiles(r).start()
    size_ref[...] = jnp.full(size_ref.shape, batch_ref[0], jnp.int32)
    leave_size = pltpu.make_async_copy(size_ref, size_hbm, leave.at[owners])
    leave_size.start()
    table[:, table_hbm.shape[1] :] = jnp.zeros((width, BLOCK), table.dtype)
    read_blocks(ids_ref, vector, which, load.at[owners])
    load_table.wait()
    for r in range(together, owners):
        load_tiles(r).start()

    def aggregated(d):
        count = counts_ref[0, d]
        left = []
        for s in range(slots):
            used = s < count
            n = lists_ref[s, 0, d]
            w = jnp.where(used, which[0, n], blocks)
            source = in_run_order(block_of(table, w), ids_ref[pl.ds(n, 1), :])
            ones = jnp.full((16, BLOCK), jnp.where(used, 1.0, 0.0), jnp.float32).astype(jnp.bfloat16)
            left.append(jnp.concatenate([source, ones], axis=0))
        right = jnp.concatenate([tiles[d, s] for s in range(slots)], axis=1)
        total = dot(right, jnp.concatenate(left, axis=1), NT).T
        return (total[:width] * (1.0 / total[width : width + 1])).astype(jnp.bfloat16)

    def some(i, carry):
        for k in range(together):
            load_tiles(i * together + k).wait()
        first = i * together * per
        results = [aggregated(first + k) for k in range(together * per)]
        own = [block_of(table, which[0, first + k]) for k in range(together * per)]
        for k in range(together * per):
            r, columns = i * together + k // per, slice((k % per) * BLOCK, (k % per + 1) * BLOCK)
            rows[r, :width, columns] = own[k]
            rows[r, width:, columns] = results[k]
        for k in range(together):
            r = i * together + k
            pltpu.make_async_copy(rows.at[r], out_hbm.at[r], leave.at[r]).start()
        return carry

    lax.fori_loop(0, dst_blocks // per // together, some, 0)
    for r in range(owners):
        pltpu.make_async_copy(rows.at[r], out_hbm.at[r], leave.at[r]).wait()
    leave_size.wait()


def outgoing(batch, lists, counts, ids, table, tiles, owners):
    width, rows = table.shape
    blocks = rows // BLOCK
    smem, vmem = pl.BlockSpec(memory_space=pltpu.SMEM), pl.BlockSpec(memory_space=pltpu.VMEM)
    anywhere = pl.BlockSpec(memory_space=pl.ANY)
    out = (owners, 2 * width, tiles.shape[0] // owners * BLOCK)
    return pl.pallas_call(
        outgoing_kernel,
        in_specs=[smem, smem, smem, vmem, anywhere, anywhere],
        out_specs=[anywhere, anywhere],
        out_shape=[jax.ShapeDtypeStruct(out, jnp.bfloat16), jax.ShapeDtypeStruct((8, BLOCK), jnp.int32)],
        scratch_shapes=[
            pltpu.VMEM(out, jnp.bfloat16),
            pltpu.VMEM((8, BLOCK), jnp.int32),
            pltpu.VMEM((width, rows + BLOCK), jnp.bfloat16),
            pltpu.VMEM(tiles.shape, jnp.bfloat16),
            pltpu.VMEM((8, blocks), jnp.int32),
            pltpu.SMEM((8, blocks), jnp.int32),
            pltpu.SemaphoreType.DMA((owners + 2,)),
            pltpu.SemaphoreType.DMA((owners + 1,)),
        ],
        compiler_params=pltpu.CompilerParams(vmem_limit_bytes=WHOLE),
        cost_estimate=pl.CostEstimate(flops=4_000_000_000, bytes_accessed=20 * MIB, transcendentals=0),
        name="pick_and_aggregate",
    )(batch, lists, counts, ids, table, tiles)


def gelu_and_slope(pre):
    c, k = 0.7978845608028654, 0.044715
    square = pre * pre
    t = jnp.tanh(c * pre * (1.0 + k * square))
    half = 0.5 * (1.0 + t)
    slope = half + 0.5 * pre * (1.0 - t * t) * (c * (1.0 + 3.0 * k * square))
    return pre * half, slope


def move_lanes(rows, order):
    order = jnp.broadcast_to(order, (8, BLOCK))
    moved = [jnp.take_along_axis(rows[i : i + 8], order, axis=1) for i in range(0, rows.shape[0], 8)]
    return jnp.concatenate(moved, axis=0)


def grads(k, moved_ref, slope, out_ref):
    owners, share, hidden = out_ref.shape
    start = pl.multiple_of(k * share, share)
    group = 4
    for i in range(0, owners, group):
        left = moved_ref[i : i + group, pl.ds(start, share), :].reshape(group * share, -1)
        out_ref[i : i + group] = dot(left, slope, NT).reshape(group, share, hidden).astype(out_ref.dtype)


def finish_kernel(
    size_ref, bias_ref, ids_ref, moved_ref, self_ref, neigh_ref, upstream_ref, hidden_ref, slope_ref, send_ref,
    turned, slopes,
):
    owners, share, hidden = send_ref.shape
    owned = moved_ref.shape[2]
    features = owners * share
    per = owned // BLOCK
    rank, core = lax.axis_index(FEAT), lax.axis_index("core")
    limit = size_ref[:1, :] - rank * owned

    lanes = lax.broadcasted_iota(jnp.int32, (8, BLOCK), 1).astype(jnp.bfloat16)
    mine = ids_ref[pl.ds(pl.multiple_of(rank * per, per), per), :]
    orders = [jnp.bitwise_and(mine[b : b + 1, :], BLOCK - 1) for b in range(per)]
    inverse = [dot(lanes, selector(order), NT).astype(jnp.int32) for order in orders]
    offset = jnp.broadcast_to(bias_ref[...], (BLOCK, hidden)).T
    turned[0] = self_ref[...].T
    turned[1] = neigh_ref[...].T

    for b in range(per):
        columns = slice(b * BLOCK, (b + 1) * BLOCK)
        own = dot(turned[0], moved_ref[:, :share, columns].reshape(features, BLOCK))
        pre = move_lanes(own, orders[b]) + offset
        pre = pre + dot(turned[1], moved_ref[:, share:, columns].reshape(features, BLOCK))
        active, back = gelu_and_slope(pre)
        positions = b * BLOCK + lax.broadcasted_iota(jnp.int32, (1, BLOCK), 1)
        valid = jnp.where(positions < limit, 1.0, 0.0)
        hidden_ref[:, columns] = (active * valid).astype(jnp.bfloat16)
        upstream = upstream_ref[columns, :].astype(jnp.float32).T
        slope = (upstream * back * valid).astype(jnp.bfloat16)
        slopes[1, :, columns] = slope
        slopes[0, :, columns] = move_lanes(slope.astype(jnp.float32), inverse[b]).astype(jnp.bfloat16)

    grads(1 - core, moved_ref, slopes[1 - core], send_ref)
    slope_ref[...] = slopes[core]


def keep_kernel(moved_ref, slope_ref, keep_ref):
    grads(lax.axis_index("core"), moved_ref, slope_ref[...], keep_ref)


def finish(size, bias, ids, moved, w_self, w_neigh, upstream):
    owners, share, owned = moved.shape[0], moved.shape[1] // 2, moved.shape[2]
    features, hidden = w_self.shape
    part = (owners, share, hidden)
    vmem = pl.BlockSpec(memory_space=pltpu.VMEM)
    return pl.pallas_call(
        finish_kernel,
        in_specs=[vmem] * 7,
        out_specs=[vmem] * 3,
        out_shape=[
            jax.ShapeDtypeStruct((hidden, owned), jnp.bfloat16),
            jax.ShapeDtypeStruct((hidden, owned), jnp.bfloat16),
            jax.ShapeDtypeStruct(part, jnp.bfloat16),
        ],
        scratch_shapes=[
            pltpu.VMEM((2, hidden, features), jnp.bfloat16),
            pltpu.VMEM((2, hidden, owned), jnp.bfloat16),
        ],
        compiler_params=pltpu.CompilerParams(vmem_limit_bytes=24 * MIB),
        cost_estimate=pl.CostEstimate(flops=2_000_000_000, bytes_accessed=9 * MIB, transcendentals=262144),
        name="finish",
    )(size, bias, ids, moved, w_self, w_neigh, upstream)


def keep_part(moved, slope):
    vmem = pl.BlockSpec(memory_space=pltpu.VMEM)
    part = (moved.shape[0], moved.shape[1] // 2, slope.shape[0])
    return pl.pallas_call(
        keep_kernel,
        in_specs=[vmem] * 2,
        out_specs=vmem,
        out_shape=jax.ShapeDtypeStruct(part, jnp.float32),
        compiler_params=pltpu.CompilerParams(vmem_limit_bytes=24 * MIB),
        cost_estimate=pl.CostEstimate(flops=1_000_000_000, bytes_accessed=4 * MIB, transcendentals=0),
        name="kept_gradient",
    )(moved, slope)


def on_device(
    node_table, node_ids, block_lists, block_counts, tiles, batch_sizes, w_self, w_neigh, bias, cotangent
):
    owners = lax.axis_size(FEAT)
    core = lax.axis_index("core")
    table = jnp.swapaxes(node_table[0], 0, 1)
    ids = node_ids[0].reshape(-1, BLOCK)

    lists = jnp.transpose(block_lists, (2, 0, 1))
    rows, size = outgoing(batch_sizes, lists, block_counts, ids, table, tiles[0], owners)
    moved = lax.all_to_all(rows, FEAT, split_axis=0, concat_axis=0, tiled=True)
    hidden, slope, send = finish(size, bias[None], ids, moved, w_self, w_neigh, cotangent[0])

    got = lax.ppermute(send, "core", [(0, 1), (1, 0)])
    keep = keep_part(moved, slope)
    parts = lax.all_to_all((keep + got).astype(jnp.bfloat16), FEAT, split_axis=0, concat_axis=0, tiled=True)
    total = jnp.sum(parts, axis=0, dtype=jnp.float32)
    others = [lax.ppermute(total, "x", [(i, (i + k) % 4) for i in range(4)]) for k in (3, 1, 2)]
    total = (total + others[2]) + (others[0] + others[1])
    other = lax.ppermute(total, "core", [(0, 1), (1, 0)])
    first_core = core == 0
    return (
        hidden.T[None],
        jnp.where(first_core, total, other),
        jnp.where(first_core, other, total),
    )


def solution(mesh):
    axes = Mesh(mesh.devices.reshape(4, 4, 4, 2), ("z", "y", "x", "core"))
    in_specs = (
        P(GRP, None, FEAT),
        P(GRP, None),
        P(GRP, None, None),
        P(GRP, None),
        P(GRP, None, None, None, None),
        P(GRP),
        P(),
        P(),
        P(),
        P(GRP, FEAT, None),
    )
    out_specs = (P(GRP, FEAT, None), P(FEAT, None), P(FEAT, None))
    return jax.shard_map(on_device, mesh=axes, in_specs=in_specs, out_specs=out_specs, check_vma=False)
```

```python
import jax
import jax.numpy as jnp
from jax import lax
from jax.experimental import pallas as pl
from jax.experimental.pallas import tpu as pltpu
from jax.sharding import Mesh, PartitionSpec as P

BLOCK = 128
MIB = 1 << 20
WHOLE = 60 * MIB
FEAT = ("z", "y")
GRP = ("x", "core")
NT = (((1,), (1,)), ((), ()))
NN = (((1,), (0,)), ((), ()))


def dot(left, right, dims=NN):
    return lax.dot_general(left, right, dims, preferred_element_type=jnp.float32)


def selector(within):
    rows = lax.broadcasted_iota(jnp.int32, (BLOCK, BLOCK), 0)
    return jnp.where(rows == within, 1.0, 0.0).astype(jnp.bfloat16)


def read_blocks(ids_ref, vector, which, sem):
    lanes = lax.broadcasted_iota(jnp.int32, (vector.shape[0], BLOCK), 1)
    first = jnp.where(lanes == 0, 1.0, 0.0).astype(jnp.bfloat16)
    blocks = lax.shift_right_logical(ids_ref[...], 7).astype(jnp.float32).astype(jnp.bfloat16)
    vector[...] = dot(first, blocks, NT).astype(jnp.int32)
    copy = pltpu.make_async_copy(vector, which, sem)
    copy.start()
    copy.wait()


def block_of(table, w):
    return table[:, pl.ds(pl.multiple_of(w * BLOCK, BLOCK), BLOCK)]


def in_run_order(chosen, ids_row):
    within = jnp.broadcast_to(jnp.bitwise_and(ids_row, BLOCK - 1), (8, BLOCK))
    chosen = chosen.astype(jnp.float32)
    rows = [jnp.take_along_axis(chosen[i : i + 8], within, axis=1) for i in range(0, chosen.shape[0], 8)]
    return jnp.concatenate(rows, axis=0).astype(jnp.bfloat16)


def outgoing_kernel(
    batch_ref, lists_ref, counts_ref, ids_ref, table_hbm, tiles_hbm, out_hbm, size_hbm, rows, size_ref, table, tiles, vector, which, load, leave
):
    blocks = ids_ref.shape[0]
    owners, width, owned = rows.shape
    width = width // 2
    per = owned // BLOCK
    slots, dst_blocks = lists_ref.shape[0], lists_ref.shape[2]
    together = 4

    def load_tiles(r):
        part = pl.ds(r * per, per)
        return pltpu.make_async_copy(tiles_hbm.at[part], tiles.at[part], load.at[r])

    known = table.at[:, pl.ds(0, table_hbm.shape[1])]
    load_table = pltpu.make_async_copy(table_hbm, known, load.at[owners + 1])
    load_table.start()
    for r in range(together):
        load_tiles(r).start()
    size_ref[...] = jnp.full(size_ref.shape, batch_ref[0], jnp.int32)
    leave_size = pltpu.make_async_copy(size_ref, size_hbm, leave.at[owners])
    leave_size.start()
    table[:, table_hbm.shape[1] :] = jnp.zeros((width, BLOCK), table.dtype)
    read_blocks(ids_ref, vector, which, load.at[owners])
    load_table.wait()
    for r in range(together, owners):
        load_tiles(r).start()

    def aggregated(d):
        count = counts_ref[0, d]
        left = []
        for s in range(slots):
            used = s < count
            n = lists_ref[s, 0, d]
            w = jnp.where(used, which[0, n], blocks)
            source = in_run_order(block_of(table, w), ids_ref[pl.ds(n, 1), :])
            ones = jnp.full((16, BLOCK), jnp.where(used, 1.0, 0.0), jnp.float32).astype(jnp.bfloat16)
            left.append(jnp.concatenate([source, ones], axis=0))
        right = jnp.concatenate([tiles[d, s] for s in range(slots)], axis=1)
        total = dot(right, jnp.concatenate(left, axis=1), NT).T
        return (total[:width] * (1.0 / total[width : width + 1])).astype(jnp.bfloat16)

    def some(i, carry):
        for k in range(together):
            load_tiles(i * together + k).wait()
        first = i * together * per
        results = [aggregated(first + k) for k in range(together * per)]
        own = [block_of(table, which[0, first + k]) for k in range(together * per)]
        for k in range(together * per):
            r, columns = i * together + k // per, slice((k % per) * BLOCK, (k % per + 1) * BLOCK)
            rows[r, :width, columns] = own[k]
            rows[r, width:, columns] = results[k]
        for k in range(together):
            r = i * together + k
            pltpu.make_async_copy(rows.at[r], out_hbm.at[r], leave.at[r]).start()
        return carry

    lax.fori_loop(0, dst_blocks // per // together, some, 0)
    for r in range(owners):
        pltpu.make_async_copy(rows.at[r], out_hbm.at[r], leave.at[r]).wait()
    leave_size.wait()


def outgoing(batch, lists, counts, ids, table, tiles, owners):
    width, rows = table.shape
    blocks = rows // BLOCK
    smem, vmem = pl.BlockSpec(memory_space=pltpu.SMEM), pl.BlockSpec(memory_space=pltpu.VMEM)
    anywhere = pl.BlockSpec(memory_space=pl.ANY)
    out = (owners, 2 * width, tiles.shape[0] // owners * BLOCK)
    return pl.pallas_call(
        outgoing_kernel,
        in_specs=[smem, smem, smem, vmem, anywhere, anywhere],
        out_specs=[anywhere, anywhere],
        out_shape=[jax.ShapeDtypeStruct(out, jnp.bfloat16), jax.ShapeDtypeStruct((8, BLOCK), jnp.int32)],
        scratch_shapes=[
            pltpu.VMEM(out, jnp.bfloat16),
            pltpu.VMEM((8, BLOCK), jnp.int32),
            pltpu.VMEM((width, rows + BLOCK), jnp.bfloat16),
            pltpu.VMEM(tiles.shape, jnp.bfloat16),
            pltpu.VMEM((8, blocks), jnp.int32),
            pltpu.SMEM((8, blocks), jnp.int32),
            pltpu.SemaphoreType.DMA((owners + 2,)),
            pltpu.SemaphoreType.DMA((owners + 1,)),
        ],
        compiler_params=pltpu.CompilerParams(vmem_limit_bytes=WHOLE),
        cost_estimate=pl.CostEstimate(flops=4_000_000_000, bytes_accessed=20 * MIB, transcendentals=0),
        name="pick_and_aggregate",
    )(batch, lists, counts, ids, table, tiles)


def gelu_and_slope(pre):
    c, k = 0.7978845608028654, 0.044715
    square = pre * pre
    t = jnp.tanh(c * pre * (1.0 + k * square))
    half = 0.5 * (1.0 + t)
    slope = half + 0.5 * pre * (1.0 - t * t) * (c * (1.0 + 3.0 * k * square))
    return pre * half, slope


def move_lanes(rows, order):
    order = jnp.broadcast_to(order, (8, BLOCK))
    moved = [jnp.take_along_axis(rows[i : i + 8], order, axis=1) for i in range(0, rows.shape[0], 8)]
    return jnp.concatenate(moved, axis=0)


def grads(k, moved_ref, slope, out_ref):
    owners, share, hidden = out_ref.shape
    start = pl.multiple_of(k * share, share)
    group = 4
    for i in range(0, owners, group):
        left = moved_ref[i : i + group, pl.ds(start, share), :].reshape(group * share, -1)
        out_ref[i : i + group] = dot(left, slope, NT).reshape(group, share, hidden).astype(out_ref.dtype)


def finish_kernel(
    size_ref, bias_ref, ids_ref, moved_ref, self_ref, neigh_ref, upstream_ref, hidden_ref, slope_ref, send_ref,
    turned, slopes,
):
    owners, share, hidden = send_ref.shape
    owned = moved_ref.shape[2]
    features = owners * share
    per = owned // BLOCK
    rank, core = lax.axis_index(FEAT), lax.axis_index("core")
    limit = size_ref[:1, :] - rank * owned

    lanes = lax.broadcasted_iota(jnp.int32, (8, BLOCK), 1).astype(jnp.bfloat16)
    mine = ids_ref[pl.ds(pl.multiple_of(rank * per, per), per), :]
    orders = [jnp.bitwise_and(mine[b : b + 1, :], BLOCK - 1) for b in range(per)]
    inverse = [dot(lanes, selector(order), NT).astype(jnp.int32) for order in orders]
    offset = jnp.broadcast_to(bias_ref[...], (BLOCK, hidden)).T
    turned[0] = self_ref[...].T
    turned[1] = neigh_ref[...].T

    for b in range(per):
        columns = slice(b * BLOCK, (b + 1) * BLOCK)
        own = dot(turned[0], moved_ref[:, :share, columns].reshape(features, BLOCK))
        pre = move_lanes(own, orders[b]) + offset
        pre = pre + dot(turned[1], moved_ref[:, share:, columns].reshape(features, BLOCK))
        active, back = gelu_and_slope(pre)
        positions = b * BLOCK + lax.broadcasted_iota(jnp.int32, (1, BLOCK), 1)
        valid = jnp.where(positions < limit, 1.0, 0.0)
        hidden_ref[:, columns] = (active * valid).astype(jnp.bfloat16)
        upstream = upstream_ref[columns, :].astype(jnp.float32).T
        slope = (upstream * back * valid).astype(jnp.bfloat16)
        slopes[1, :, columns] = slope
        slopes[0, :, columns] = move_lanes(slope.astype(jnp.float32), inverse[b]).astype(jnp.bfloat16)

    grads(1 - core, moved_ref, slopes[1 - core], send_ref)
    slope_ref[...] = slopes[core]


def keep_kernel(moved_ref, slope_ref, hidden_ref, keep_ref, turned_ref):
    turned_ref[...] = hidden_ref[...].T
    grads(lax.axis_index("core"), moved_ref, slope_ref[...], keep_ref)


def finish(size, bias, ids, moved, w_self, w_neigh, upstream):
    owners, share, owned = moved.shape[0], moved.shape[1] // 2, moved.shape[2]
    features, hidden = w_self.shape
    part = (owners, share, hidden)
    vmem = pl.BlockSpec(memory_space=pltpu.VMEM)
    return pl.pallas_call(
        finish_kernel,
        in_specs=[vmem] * 7,
        out_specs=[vmem] * 3,
        out_shape=[
            jax.ShapeDtypeStruct((hidden, owned), jnp.bfloat16),
            jax.ShapeDtypeStruct((hidden, owned), jnp.bfloat16),
            jax.ShapeDtypeStruct(part, jnp.bfloat16),
        ],
        scratch_shapes=[
            pltpu.VMEM((2, hidden, features), jnp.bfloat16),
            pltpu.VMEM((2, hidden, owned), jnp.bfloat16),
        ],
        compiler_params=pltpu.CompilerParams(vmem_limit_bytes=24 * MIB),
        cost_estimate=pl.CostEstimate(flops=2_000_000_000, bytes_accessed=9 * MIB, transcendentals=262144),
        name="finish",
    )(size, bias, ids, moved, w_self, w_neigh, upstream)


def keep_part(moved, slope, hidden):
    vmem = pl.BlockSpec(memory_space=pltpu.VMEM)
    part = (moved.shape[0], moved.shape[1] // 2, slope.shape[0])
    return pl.pallas_call(
        keep_kernel,
        in_specs=[vmem] * 3,
        out_specs=[vmem] * 2,
        out_shape=[
            jax.ShapeDtypeStruct(part, jnp.float32),
            jax.ShapeDtypeStruct(hidden.shape[::-1], hidden.dtype),
        ],
        compiler_params=pltpu.CompilerParams(vmem_limit_bytes=24 * MIB),
        cost_estimate=pl.CostEstimate(flops=1_000_000_000, bytes_accessed=4 * MIB, transcendentals=0),
        name="kept_gradient",
    )(moved, slope, hidden)


def on_device(
    node_table, node_ids, block_lists, block_counts, tiles, batch_sizes, w_self, w_neigh, bias, cotangent
):
    owners = lax.axis_size(FEAT)
    core = lax.axis_index("core")
    table = jnp.swapaxes(node_table[0], 0, 1)
    ids = node_ids[0].reshape(-1, BLOCK)

    lists = jnp.transpose(block_lists, (2, 0, 1))
    rows, size = outgoing(batch_sizes, lists, block_counts, ids, table, tiles[0], owners)
    moved = lax.all_to_all(rows, FEAT, split_axis=0, concat_axis=0, tiled=True)
    hidden, slope, send = finish(size, bias[None], ids, moved, w_self, w_neigh, cotangent[0])

    got = lax.ppermute(send, "core", [(0, 1), (1, 0)])
    keep, hidden = keep_part(moved, slope, hidden)
    parts = lax.all_to_all((keep + got).astype(jnp.bfloat16), FEAT, split_axis=0, concat_axis=0, tiled=True)
    total = jnp.sum(parts, axis=0, dtype=jnp.float32)
    others = [lax.ppermute(total, "x", [(i, (i + k) % 4) for i in range(4)]) for k in (3, 1, 2)]
    total = (total + others[2]) + (others[0] + others[1])
    other = lax.ppermute(total, "core", [(0, 1), (1, 0)])
    first_core = core == 0
    return (
        hidden[None],
        jnp.where(first_core, total, other),
        jnp.where(first_core, other, total),
    )


def solution(mesh):
    axes = Mesh(mesh.devices.reshape(4, 4, 4, 2), ("z", "y", "x", "core"))
    in_specs = (
        P(GRP, None, FEAT),
        P(GRP, None),
        P(GRP, None, None),
        P(GRP, None),
        P(GRP, None, None, None, None),
        P(GRP),
        P(),
        P(),
        P(),
        P(GRP, FEAT, None),
    )
    out_specs = (P(GRP, FEAT, None), P(FEAT, None), P(FEAT, None))
    return jax.shard_map(on_device, mesh=axes, in_specs=in_specs, out_specs=out_specs, check_vma=False)
```
